32 devices in a mesh: cam: 4 (over y, core), frame: 8 (over z, x).
Axes of the slice: x: 2, y: 2, z: 4, core: 2. Of those that a mesh axis runs over, the one named last changes fastest.
Arguments:
- tokens: bfloat16 [8, 8, 256, 1152], P('cam', 'frame'), may hold values from -6 to 6
- counts: int32 [8, 8], P('cam', 'frame'), may hold values from 1 to 4, as said below
- neighbours: int32 [8, 2], P('cam'), may hold values from 0 to 7, as said below
- side_keys: bfloat16 [2, 576], replicated, may hold values from -5 to 5
- cross_qkv: bfloat16 [1152, 1728], replicated, may hold values from -2 to 2
- cross_out: bfloat16 [576, 1152], replicated, may hold values from -0.25 to 0.25
- time_qkv: bfloat16 [1152, 1728], replicated, may hold values from -2 to 2
- time_out: bfloat16 [576, 1152], replicated, may hold values from -0.25 to 0.25
Outputs:
- block_output: bfloat16 [8, 8, 256, 1152], P('cam', 'frame')
The draws below stay inside these ranges and needn't reach their ends.
Inputs may be any that keep to these rules, and one draw needn't show every extreme that they name: `counts`: in every camera some frame is full, with 4 rows. Row c holds camera c's cycle neighbours (c - 1) mod 8 and (c + 1) mod 8, in either order.
All inputs are finite; a program needn't handle non-finite values.
Results may differ from the reference program's by a relative error of at most 0.017.
The reference program's roundings to bfloat16 on the way count: a program that leaves them out, or rounds other values in their place, can miss the bound.
Values may be sent and summed in bfloat16 or wider, within the bound.
A program may use at most 128 MiB of HBM per device.

```python
import jax
import jax.numpy as jnp
from jax import lax

D = 1152
HEADS = 8
HEAD_DIM = 72
INNER = 576
TOK = 256
CAMS = 8
FRAMES = 8


def weight_matrix(key, strength):
    spread = (D // 4) ** (-0.5)
    shape = (D, 3 * INNER)
    key = jax.random.fold_in(key, strength)
    result = jnp.clip(jax.random.normal(key, shape, jnp.float32), -6.0, 6.0) * spread
    return result


def draw_cross_qkv(key, part):
    return weight_matrix(key, 300).astype(jnp.bfloat16)


def draw_time_qkv(key, part):
    return weight_matrix(key, 600).astype(jnp.bfloat16)


def draw_tokens(key, part):
    shape = (CAMS, FRAMES, TOK, D)
    key = jax.random.fold_in(key, 5)
    result = jnp.clip(jax.random.normal(key, shape, jnp.float32), -6.0, 6.0)
    return result.astype(jnp.bfloat16)


def draw_counts(key, part):
    key = jax.random.fold_in(key, 11)
    first_key, second_key = jax.random.split(key)
    most_rows = TOK // 64
    base = jax.random.randint(first_key, (CAMS, FRAMES), 1, most_rows + 1)
    full_frame = jax.random.randint(second_key, (CAMS, 1), 0, FRAMES)
    frame_ids = jnp.arange(FRAMES, dtype=jnp.int32)[None, :]
    return jnp.where(frame_ids == full_frame, most_rows, base).astype(jnp.int32)


def draw_neighbours(key, part):
    key = jax.random.fold_in(key, 23)
    flips = jax.random.randint(key, (CAMS,), 0, 2)
    cam_ids = jnp.arange(CAMS, dtype=jnp.int32)
    lower = (cam_ids - 1) % CAMS
    upper = (cam_ids + 1) % CAMS
    first = jnp.where(flips == 1, upper, lower)
    second = jnp.where(flips == 1, lower, upper)
    return jnp.stack([first, second], axis=1).astype(jnp.int32)


def scatter_about(own_key, dims, scale, most, kind=jnp.bfloat16):
    return jnp.clip(scale * jax.random.normal(own_key, dims, jnp.float32), -most, most).astype(kind)


def setup_inputs(seed: int = 0) -> dict:
    splits = jax.random.split(jax.random.key(seed), 9)
    tokens = draw_tokens(jax.random.fold_in(splits[8], 71), 0)
    counts = draw_counts(jax.random.fold_in(splits[8], 71), 0)
    neighbours = draw_neighbours(jax.random.fold_in(splits[8], 71), 0)
    side_keys = scatter_about(splits[3], (2, INNER), 1.0, 5.0)
    cross_qkv = draw_cross_qkv(jax.random.fold_in(splits[8], 71), 0)
    cross_out = scatter_about(splits[5], (INNER, D), INNER ** -0.5, 0.25)
    time_qkv = draw_time_qkv(jax.random.fold_in(splits[8], 71), 0)
    time_out = scatter_about(splits[7], (INNER, D), INNER ** -0.5, 0.25)
    return dict(tokens=tokens, counts=counts, neighbours=neighbours, side_keys=side_keys, cross_qkv=cross_qkv, cross_out=cross_out, time_qkv=time_qkv, time_out=time_out)


epsilon = 1e-06
row_tokens = 64

def normalize(values):
    values = values.astype(jnp.float32)
    mean = lax.optimization_barrier(jnp.mean(values, axis=-1, keepdims=True))
    centred = values - mean
    variance = lax.optimization_barrier(jnp.mean(centred * centred, axis=-1, keepdims=True))
    return (centred * lax.rsqrt(variance + epsilon)).astype(jnp.bfloat16)

def project(normed, weight):
    flat = normed.reshape(-1, normed.shape[-1])
    result = jnp.dot(flat, weight, preferred_element_type=jnp.float32)
    return result.reshape(normed.shape[:-1] + (weight.shape[1],))

def softmax_rows(scores, allowed):
    masked = jnp.where(allowed, scores, -1e+30)
    highest = lax.optimization_barrier(jnp.max(masked, axis=-1, keepdims=True))
    expo = jnp.exp(masked - highest)
    return (expo / lax.optimization_barrier(jnp.sum(expo, axis=-1, keepdims=True))).astype(jnp.bfloat16)

def reference(tokens, counts, neighbours, side_keys, cross_qkv, cross_out, time_qkv, time_out):
    cameras, frames, token_count, width = tokens.shape
    inner = HEADS * HEAD_DIM
    scale = HEAD_DIM ** (-0.5)
    position = jnp.arange(token_count, dtype=jnp.int32)
    valid = position[None, None, :] < row_tokens * counts[:, :, None]

    def cross_project(camera_tokens):
        return project(normalize(camera_tokens), cross_qkv).astype(jnp.bfloat16)
    projected = lax.map(cross_project, tokens)
    query = projected[..., :inner]
    keys = projected[..., inner:2 * inner]
    values = projected[..., 2 * inner:]
    cam_ids = jnp.arange(cameras, dtype=jnp.int32)
    lower = (cam_ids - 1) % cameras
    upper = (cam_ids + 1) % cameras
    first_lower = neighbours[:, 0] == lower
    side_lower = jnp.where(first_lower[:, None], side_keys[0][None], side_keys[1][None]).astype(jnp.float32)
    side_upper = jnp.where(first_lower[:, None], side_keys[1][None], side_keys[0][None]).astype(jnp.float32)
    lower_keys = (keys[lower].astype(jnp.float32) + side_lower[:, None, None, :]).astype(jnp.bfloat16)
    upper_keys = (keys[upper].astype(jnp.float32) + side_upper[:, None, None, :]).astype(jnp.bfloat16)
    all_keys = jnp.concatenate([keys, lower_keys, upper_keys], axis=2)
    all_values = jnp.concatenate([values, values[lower], values[upper]], axis=2)
    all_valid = jnp.concatenate([valid, valid[lower], valid[upper]], axis=2)

    def cross_one(pieces):
        one_query, one_keys, one_values, one_valid = pieces
        query_heads = one_query.reshape(token_count, HEADS, HEAD_DIM).astype(jnp.float32)
        key_heads = one_keys.reshape(3 * token_count, HEADS, HEAD_DIM).astype(jnp.float32)
        value_heads = one_values.reshape(3 * token_count, HEADS, HEAD_DIM).astype(jnp.float32)
        scores = jnp.einsum('qhd,khd->hqk', query_heads, key_heads) * scale
        probs = softmax_rows(scores, one_valid[None, None, :])
        attended = jnp.einsum('hqk,khd->qhd', probs.astype(jnp.float32), value_heads)
        return attended.reshape(token_count, inner).astype(jnp.bfloat16)
    flat_count = cameras * frames
    attended = lax.map(cross_one, (query.reshape(flat_count, token_count, inner), all_keys.reshape(flat_count, 3 * token_count, inner), all_values.reshape(flat_count, 3 * token_count, inner), all_valid.reshape(flat_count, 3 * token_count)))
    attended = attended.reshape(cameras, frames, token_count, inner)
    mixed = (project(attended, cross_out) + tokens.astype(jnp.float32)).astype(jnp.bfloat16)

    def time_project(camera_tokens):
        return project(normalize(camera_tokens), time_qkv).astype(jnp.bfloat16)
    time_proj = lax.map(time_project, mixed)
    same_frame = jnp.eye(frames, dtype=jnp.bool_)

    def time_one(pieces):
        one_proj, one_valid = pieces
        query_heads = one_proj[..., :inner].reshape(frames, token_count, HEADS, HEAD_DIM).astype(jnp.float32)
        key_heads = one_proj[..., inner:2 * inner].reshape(frames, token_count, HEADS, HEAD_DIM).astype(jnp.float32)
        value_heads = one_proj[..., 2 * inner:].reshape(frames, token_count, HEADS, HEAD_DIM).astype(jnp.float32)
        scores = jnp.einsum('fthd,gthd->thfg', query_heads, key_heads) * scale
        allowed = jnp.transpose(one_valid)[:, None, None, :] | same_frame[None, None]
        probs = softmax_rows(scores, allowed)
        attended_time = jnp.einsum('thfg,gthd->fthd', probs.astype(jnp.float32), value_heads)
        return attended_time.reshape(frames, token_count, inner).astype(jnp.bfloat16)
    time_attended = lax.map(time_one, (time_proj, valid))
    result = project(time_attended, time_out) + mixed.astype(jnp.float32)
    return result.astype(jnp.bfloat16)
```

```python
import functools
import math

import jax
import jax.numpy as jnp
from jax import lax
from jax.experimental import pallas as pl
from jax.experimental.pallas import tpu as pltpu
from jax.sharding import PartitionSpec as P

HEADS = 8
MESH = pl.DeviceIdType.MESH

epsilon = 1e-06
row_tokens = 64
minus = -1e30


def normalize(values):
    values = values.astype(jnp.float32)
    mean = jnp.mean(values, axis=-1, keepdims=True)
    centred = values - mean
    variance = jnp.mean(centred * centred, axis=-1, keepdims=True)
    return (centred * lax.rsqrt(variance + epsilon)).astype(jnp.bfloat16)


def dot(a, b):
    return jnp.dot(a, b, preferred_element_type=jnp.float32)


def dot_t(a, b):
    return lax.dot_general(a, b, (((1,), (1,)), ((), ())), preferred_element_type=jnp.float32)


class Heads:
    def __init__(self, inner):
        self.inner = inner
        self.size = inner // HEADS
        self.scale = self.size ** (-0.5) * math.log2(math.e)
        self.windows = []
        for h in range(HEADS):
            lo = h * self.size
            start = lo // 128 * 128
            end = min(-(-(lo + self.size) // 128) * 128, inner)
            self.windows.append((start, end))

    def mask(self, h, dtype):
        start, end = self.windows[h]
        lane = lax.broadcasted_iota(jnp.int32, (1, end - start), 1) + start
        inside = (lane >= h * self.size) & (lane < (h + 1) * self.size)
        return jnp.where(inside, 1.0, 0.0).astype(dtype)

    def gather(self, results):
        tiles = {}
        for h, result in enumerate(results):
            start, end = self.windows[h]
            for at in range(start, end, 128):
                piece = result[:, at - start : min(at + 128, end) - start]
                tiles[at] = tiles[at] + piece if at in tiles else piece
        return jnp.concatenate([tiles[at] for at in sorted(tiles)], axis=1)


def block_kernel(
    peers,
    cam_peers,
    counts,
    neighbours,
    tokens_hbm,
    side_keys,
    cross_qkv_hbm,
    cross_out_hbm,
    time_qkv_hbm,
    time_out_hbm,
    out,
    tokens,
    cross_qkv,
    cross_out,
    time_qkv,
    time_out,
    edge,
    query,
    keys,
    values,
    shifted,
    sides,
    far_values,
    part,
    highest,
    total,
    mixed,
    leaving,
    arrived,
    attended,
    returned,
    count_out,
    count_in,
    count_edge,
    load_sem,
    edge_send,
    edge_recv,
    count_send,
    count_recv,
    cedge_send,
    cedge_recv,
    go_send,
    go_recv,
    back_send,
    back_recv,
):
    cams, token_count, width = tokens.shape
    inner = cross_out.shape[0]
    heads = Heads(inner)
    rows = token_count // peers
    me = lax.axis_index("frame")
    cam = lax.axis_index("cam")
    above = lax.rem(cam + 1, cam_peers)
    below = lax.rem(cam + cam_peers - 1, cam_peers)
    others = [lax.rem(me + k, peers) for k in range(1, peers)]

    loads = [
        pltpu.make_async_copy(source, target, load_sem.at[i])
        for i, (source, target) in enumerate(
            (
                (tokens_hbm, tokens),
                (cross_qkv_hbm, cross_qkv),
                (cross_out_hbm, cross_out),
                (time_qkv_hbm, time_qkv),
                (time_out_hbm, time_out),
            )
        )
    ]
    for load in loads:
        load.start()

    for c in range(cams):
        count_out[pl.ds(c, 1), :] = jnp.full((1, token_count), counts[c, 0], jnp.int32)

    barrier = pltpu.get_barrier_semaphore()
    for peer in others:
        pl.semaphore_signal(barrier, inc=1, device_id={"frame": peer}, device_id_type=MESH)
    for peer in (above, below):
        pl.semaphore_signal(barrier, inc=1, device_id={"cam": peer}, device_id_type=MESH)
    pl.semaphore_wait(barrier, peers + 1)

    def remote(source, target, send, recv, device):
        return pltpu.make_async_remote_copy(
            src_ref=source,
            dst_ref=target,
            send_sem=send,
            recv_sem=recv,
            device_id=device,
            device_id_type=MESH,
        )

    edges = []
    for slot, peer in ((0, above), (1, below)):
        copy = remote(
            tokens_hbm.at[1 - slot],
            edge.at[slot],
            edge_send.at[slot],
            edge_recv.at[slot],
            {"cam": peer},
        )
        copy.start()
        edges.append(copy)
    for slot, peer in ((0, above), (1, below)):
        copy = remote(
            count_out,
            count_edge.at[slot],
            cedge_send.at[slot],
            cedge_recv.at[slot],
            {"cam": peer},
        )
        copy.start()
        edges.append(copy)

    def count_copy(peer):
        return remote(
            count_out, count_in.at[me], count_send.at[peer], count_recv.at[me], {"frame": peer}
        )

    for peer in others:
        count_copy(peer).start()
    count_in[me] = count_out[...]

    cameras = cams * cam_peers
    first = side_keys[0:1, :].astype(jnp.float32)
    second = side_keys[1:2, :].astype(jnp.float32)
    for c in range(cams):
        lower = lax.rem(cams * cam + c + cameras - 1, cameras)
        straight = jnp.where(neighbours[c, 0] == lower, 1.0, 0.0)
        side_lower = first * straight + second * (1.0 - straight)
        side_upper = second * straight + first * (1.0 - straight)
        near, far = (side_upper, side_lower) if c == 0 else (side_lower, side_upper)
        sides[pl.ds(c, 1), :] = near
        sides[pl.ds(cams + c, 1), :] = far

    aligned = inner // 128 * 128

    def key_value(normed, weight):
        key = dot(normed, weight[:, aligned : 2 * inner])[:, inner - aligned :]
        value = dot(normed, weight[:, 2 * inner :])
        return key, value.astype(jnp.bfloat16)

    loads[0].wait()
    normed = normalize(tokens[...].reshape(cams * token_count, width))
    loads[1].wait()
    shape = (cams, token_count, inner)
    query[...] = dot(normed, cross_qkv[:, :inner]).astype(jnp.bfloat16).reshape(shape)
    key, value = key_value(normed, cross_qkv)
    keys[...] = key.astype(jnp.bfloat16).reshape(shape)
    values[...] = value.reshape(shape)

    def bias_of(row):
        lane = lax.broadcasted_iota(jnp.int32, row.shape, 1)
        return jnp.where(lane < row_tokens * row, 0.0, minus)

    def with_side(key, side):
        return (key.astype(jnp.float32) + side).astype(jnp.bfloat16)

    def local_part(c, carry):
        near = 1 - c
        shifted[...] = with_side(keys[near], sides[pl.ds(c, 1), :])
        own_bias = bias_of(count_out[pl.ds(c, 1), :])
        near_bias = bias_of(count_out[pl.ds(near, 1), :])
        for h in range(HEADS):
            start, end = heads.windows[h]
            q = query[c, :, start:end] * heads.mask(h, jnp.bfloat16)
            own = dot_t(q, keys[c, :, start:end]) * heads.scale + own_bias
            other = dot_t(q, shifted[:, start:end]) * heads.scale + near_bias
            top = jnp.max(jnp.maximum(own, other), axis=1, keepdims=True)
            own = jnp.exp2(own - top)
            other = jnp.exp2(other - top)
            highest[c, h] = top
            total[c, h] = jnp.sum(own + other, axis=1, keepdims=True)
            part[c, h, :, : end - start] = dot(
                own.astype(jnp.bfloat16), values[c, :, start:end]
            ) + dot(other.astype(jnp.bfloat16), values[near, :, start:end])
        return carry

    lax.fori_loop(0, cams, local_part, 0)

    def go_copy(c, peer):
        return remote(
            leaving.at[c, peer],
            arrived.at[c, me],
            go_send.at[c, peer],
            go_recv.at[c, me],
            {"frame": peer},
        )

    def back_copy(c, peer):
        return remote(
            attended.at[c, peer],
            returned.at[c, me],
            back_send.at[c, peer],
            back_recv.at[c, me],
            {"frame": peer},
        )

    def landed(buffer, sem, c, peer):
        remote(
            buffer.at[c, peer], buffer.at[c, peer], sem.at[c, peer], sem.at[c, peer], {"frame": peer}
        ).wait_recv()

    def camera_at(step):
        return lax.rem(step + cam + 1, 2)

    loads[2].wait()

    def remote_part(step, carry):
        c = camera_at(step)
        remote(
            edge.at[c], edge.at[c], edge_recv.at[c], edge_recv.at[c], {"cam": above}
        ).wait_recv()
        remote(
            count_edge.at[c], count_edge.at[c], cedge_recv.at[c], cedge_recv.at[c], {"cam": above}
        ).wait_recv()
        key, value = key_value(normalize(edge[c]), cross_qkv)
        shifted[...] = with_side(key.astype(jnp.bfloat16), sides[pl.ds(cams + c, 1), :])
        far_values[...] = value
        bias = bias_of(count_edge[c, pl.ds(1 - c, 1), :])
        results = []
        for h in range(HEADS):
            start, end = heads.windows[h]
            q = query[c, :, start:end] * heads.mask(h, jnp.bfloat16)
            scores = dot_t(q, shifted[:, start:end]) * heads.scale + bias
            before = highest[c, h]
            top = jnp.maximum(before, jnp.max(scores, axis=1, keepdims=True))
            scores = jnp.exp2(scores - top)
            shrink = jnp.exp2(before - top)
            whole = total[c, h] * shrink + jnp.sum(scores, axis=1, keepdims=True)
            result = part[c, h, :, : end - start] * shrink + dot(
                scores.astype(jnp.bfloat16), far_values[:, start:end]
            )
            results.append(result * (1.0 / whole) * heads.mask(h, jnp.float32))
        result = heads.gather(results).astype(jnp.bfloat16)
        sum_ = (dot(result, cross_out[...]) + tokens[c].astype(jnp.float32)).astype(jnp.bfloat16)
        mixed[c] = sum_
        leaving[c] = normalize(sum_).reshape(peers, rows, width)
        for peer in others:
            go_copy(c, peer).start()
        arrived[c, me] = leaving[c, me]
        return carry

    lax.fori_loop(0, cams, remote_part, 0)

    for peer in others:
        remote(
            count_in.at[peer],
            count_in.at[peer],
            count_recv.at[peer],
            count_recv.at[peer],
            {"frame": peer},
        ).wait_recv()
    loads[3].wait()

    def time_part(step, carry):
        c = camera_at(step)
        row = lax.broadcasted_iota(jnp.int32, (token_count, 1), 0)
        lane = lax.broadcasted_iota(jnp.int32, (1, token_count), 1)
        count = jnp.zeros((1, token_count), jnp.int32)
        row_frame = jnp.zeros((token_count, 1), jnp.int32)
        lane_frame = jnp.zeros((1, token_count), jnp.int32)
        for g in range(peers):
            here = (lane >= g * rows) & (lane < (g + 1) * rows)
            count = jnp.where(here, count_in[g, pl.ds(c, 1), :], count)
            if g:
                row_frame = row_frame + jnp.where(row >= g * rows, 1, 0)
                lane_frame = lane_frame + jnp.where(lane >= g * rows, 1, 0)
        place = lane - lane_frame * rows
        valid = jnp.where(me * rows + place < row_tokens * count, 1, 0)
        same_place = (row - row_frame * rows) == place
        seen = jnp.where(row_frame == lane_frame, 1, valid)
        bias = jnp.where(same_place, jnp.where(seen == 1, 0.0, minus), minus)
        for peer in others:
            landed(arrived, go_recv, c, peer)
        x = arrived[c].reshape(token_count, width)
        query[0] = dot(x, time_qkv[:, :inner]).astype(jnp.bfloat16)
        key, value = key_value(x, time_qkv)
        keys[0] = key.astype(jnp.bfloat16)
        values[0] = value
        results = []
        for h in range(HEADS):
            start, end = heads.windows[h]
            q = query[0, :, start:end] * heads.mask(h, jnp.bfloat16)
            scores = dot_t(q, keys[0, :, start:end]) * heads.scale + bias
            scores = jnp.exp2(scores - jnp.max(scores, axis=1, keepdims=True))
            whole = jnp.sum(scores, axis=1, keepdims=True)
            result = dot(scores.astype(jnp.bfloat16), values[0, :, start:end])
            results.append(result * (1.0 / whole) * heads.mask(h, jnp.float32))
        result = heads.gather(results).astype(jnp.bfloat16)
        attended[c] = result.reshape(peers, rows, inner)
        for peer in others:
            back_copy(c, peer).start()
        returned[c, me] = attended[c, me]
        return carry

    lax.fori_loop(0, cams, time_part, 0)
    loads[4].wait()

    def last_part(step, carry):
        c = camera_at(step)
        for peer in others:
            landed(returned, back_recv, c, peer)
        x = returned[c].reshape(token_count, inner)
        out[c] = (dot(x, time_out[...]) + mixed[c].astype(jnp.float32)).astype(jnp.bfloat16)
        return carry

    lax.fori_loop(0, cams, last_part, 0)

    for copy in edges:
        copy.wait_send()
    for peer in others:
        count_copy(peer).wait_send()
        for c in range(cams):
            go_copy(c, peer).wait_send()
            back_copy(c, peer).wait_send()


def whole_block(
    tokens, counts, neighbours, side_keys, cross_qkv, cross_out, time_qkv, time_out
):
    cams, frames, token_count, width = tokens.shape
    inner = cross_out.shape[0]
    peers = lax.axis_size("frame")
    cam_peers = lax.axis_size("cam")
    rows = token_count // peers
    bf16, f32 = jnp.bfloat16, jnp.float32
    vmem, smem, hbm = (
        pl.BlockSpec(memory_space=space) for space in (pltpu.VMEM, pltpu.SMEM, pl.ANY)
    )
    dma = pltpu.SemaphoreType.DMA
    scratch = [
        pltpu.VMEM((cams, token_count, width), bf16),
        pltpu.VMEM(cross_qkv.shape, bf16),
        pltpu.VMEM(cross_out.shape, bf16),
        pltpu.VMEM(time_qkv.shape, bf16),
        pltpu.VMEM(time_out.shape, bf16),
        pltpu.VMEM((2, token_count, width), bf16),
        pltpu.VMEM((cams, token_count, inner), bf16),
        pltpu.VMEM((cams, token_count, inner), bf16),
        pltpu.VMEM((cams, token_count, inner), bf16),
        pltpu.VMEM((token_count, inner), bf16),
        pltpu.VMEM((8, inner), f32),
        pltpu.VMEM((token_count, inner), bf16),
        pltpu.VMEM((cams, HEADS, token_count, 256), f32),
        pltpu.VMEM((cams, HEADS, token_count, 1), f32),
        pltpu.VMEM((cams, HEADS, token_count, 1), f32),
        pltpu.VMEM((cams, token_count, width), bf16),
        pltpu.VMEM((cams, peers, rows, width), bf16),
        pltpu.VMEM((cams, peers, rows, width), bf16),
        pltpu.VMEM((cams, peers, rows, inner), bf16),
        pltpu.VMEM((cams, peers, rows, inner), bf16),
        pltpu.VMEM((8, token_count), jnp.int32),
        pltpu.VMEM((peers, 8, token_count), jnp.int32),
        pltpu.VMEM((2, 8, token_count), jnp.int32),
        dma((5,)),
        dma((2,)),
        dma((2,)),
        dma((peers,)),
        dma((peers,)),
        dma((2,)),
        dma((2,)),
        dma((cams, peers)),
        dma((cams, peers)),
        dma((cams, peers)),
        dma((cams, peers)),
    ]
    result = pl.pallas_call(
        functools.partial(block_kernel, peers, cam_peers),
        out_shape=jax.ShapeDtypeStruct((cams, token_count, width), bf16),
        in_specs=[smem, smem, hbm, vmem, hbm, hbm, hbm, hbm],
        out_specs=vmem,
        scratch_shapes=scratch,
        compiler_params=pltpu.CompilerParams(
            collective_id=0, has_side_effects=True, vmem_limit_bytes=58 * 2**20
        ),
    )(
        counts,
        neighbours,
        tokens.reshape(cams, token_count, width),
        side_keys,
        cross_qkv,
        cross_out,
        time_qkv,
        time_out,
    )
    return result.reshape(tokens.shape)


def passed_along(x, axis, by):
    peers = lax.axis_size(axis)
    return lax.ppermute(x, axis, [(i, (i + by) % peers) for i in range(peers)])


def project(normed, weight):
    flat = normed.reshape(-1, normed.shape[-1])
    result = jnp.dot(flat, weight, preferred_element_type=jnp.float32)
    return result.reshape(normed.shape[:-1] + (weight.shape[1],))


def softmax_rows(scores, allowed):
    masked = jnp.where(allowed, scores, -1e30)
    highest = jnp.max(masked, axis=-1, keepdims=True)
    expo = jnp.exp(masked - highest)
    return (expo / jnp.sum(expo, axis=-1, keepdims=True)).astype(jnp.bfloat16)


def temporal_tail(projected, arrived, time_out):
    cams_here, frames, places, _ = projected.shape
    inner = time_out.shape[0]
    head_size = inner // HEADS
    query_heads = projected[..., :inner].reshape(cams_here, frames, places, HEADS, head_size)
    key_heads = projected[..., inner : 2 * inner].reshape(
        cams_here, frames, places, HEADS, head_size
    )
    value_heads = projected[..., 2 * inner :].reshape(cams_here, frames, places, HEADS, head_size)
    scores = jnp.einsum(
        "cfphd,cgphd->cphfg", query_heads, key_heads, preferred_element_type=jnp.float32
    ) * head_size ** (-0.5)
    allowed = (jnp.transpose(arrived, (0, 2, 1)) > 0.5)[:, :, None, None, :]
    allowed = allowed | jnp.eye(frames, dtype=jnp.bool_)[None, None, None]
    probs = softmax_rows(scores, allowed)
    attended = jnp.einsum(
        "cphfg,cgphd->cfphd", probs, value_heads, preferred_element_type=jnp.float32
    )
    attended = attended.astype(jnp.bfloat16).reshape(cams_here, frames, places, inner)
    returned = lax.all_to_all(attended, "frame", split_axis=1, concat_axis=2, tiled=True)
    return project(returned, time_out)


def plain_block(tokens, counts, neighbours, side_keys, cross_qkv, cross_out, time_qkv, time_out):
    cam_here, frames_here, token_count, width = tokens.shape
    inner = cross_out.shape[0]
    head_size = inner // HEADS
    position = lax.broadcasted_iota(jnp.int32, (cam_here, frames_here, token_count), 2)
    valid = (position < row_tokens * counts[:, :, None]).astype(jnp.bfloat16)
    projected = project(normalize(tokens), cross_qkv).astype(jnp.bfloat16)
    query = projected[..., :inner]
    keys = projected[..., inner : 2 * inner]
    values = projected[..., 2 * inner :]
    left_keys, left_values, left_valid = passed_along((keys[-1], values[-1], valid[-1]), "cam", 1)
    right_keys, right_values, right_valid = passed_along((keys[0], values[0], valid[0]), "cam", -1)
    lower_keys = jnp.concatenate([left_keys[None], keys[:-1]], axis=0)
    lower_values = jnp.concatenate([left_values[None], values[:-1]], axis=0)
    lower_valid = jnp.concatenate([left_valid[None], valid[:-1]], axis=0)
    upper_keys = jnp.concatenate([keys[1:], right_keys[None]], axis=0)
    upper_values = jnp.concatenate([values[1:], right_values[None]], axis=0)
    upper_valid = jnp.concatenate([valid[1:], right_valid[None]], axis=0)
    cameras = cam_here * lax.axis_size("cam")
    cam_ids = cam_here * lax.axis_index("cam") + jnp.arange(cam_here, dtype=jnp.int32)
    first_lower = neighbours[:, 0] == (cam_ids - 1) % cameras
    side_lower = jnp.where(first_lower[:, None], side_keys[0][None], side_keys[1][None]).astype(
        jnp.float32
    )
    side_upper = jnp.where(first_lower[:, None], side_keys[1][None], side_keys[0][None]).astype(
        jnp.float32
    )
    lower_keys = (lower_keys.astype(jnp.float32) + side_lower[:, None, None, :]).astype(
        jnp.bfloat16
    )
    upper_keys = (upper_keys.astype(jnp.float32) + side_upper[:, None, None, :]).astype(
        jnp.bfloat16
    )
    all_keys = jnp.concatenate([keys, lower_keys, upper_keys], axis=2)
    all_values = jnp.concatenate([values, lower_values, upper_values], axis=2)
    all_valid = jnp.concatenate([valid, lower_valid, upper_valid], axis=2)
    items = cam_here * frames_here
    query_heads = query.reshape(items, token_count, HEADS, head_size)
    key_heads = all_keys.reshape(items, 3 * token_count, HEADS, head_size)
    value_heads = all_values.reshape(items, 3 * token_count, HEADS, head_size)
    scores = jnp.einsum(
        "bqhd,bkhd->bhqk", query_heads, key_heads, preferred_element_type=jnp.float32
    ) * head_size ** (-0.5)
    allowed = (all_valid.reshape(items, 3 * token_count) > 0.5)[:, None, None, :]
    probs = softmax_rows(scores, allowed)
    attended = jnp.einsum("bhqk,bkhd->bqhd", probs, value_heads, preferred_element_type=jnp.float32)
    attended = attended.astype(jnp.bfloat16).reshape(cam_here, frames_here, token_count, inner)
    mixed = (project(attended, cross_out) + tokens.astype(jnp.float32)).astype(jnp.bfloat16)
    normed = lax.all_to_all(normalize(mixed), "frame", split_axis=2, concat_axis=1, tiled=True)
    temporal = temporal_tail(
        project(normed, time_qkv).astype(jnp.bfloat16),
        lax.all_to_all(valid, "frame", split_axis=2, concat_axis=1, tiled=True),
        time_out,
    )
    return (temporal + mixed.astype(jnp.float32)).astype(jnp.bfloat16)


def shards(tokens, counts, neighbours, side_keys, cross_qkv, cross_out, time_qkv, time_out):
    cams, frames, token_count, _ = tokens.shape
    peers = lax.axis_size("frame")
    fits = (
        cams == 2
        and frames == 1
        and lax.axis_size("cam") > 2
        and token_count == 256
        and token_count % (16 * peers) == 0
    )
    chosen = whole_block if fits else plain_block
    return chosen(
        tokens, counts, neighbours, side_keys, cross_qkv, cross_out, time_qkv, time_out
    )


def solution(mesh):
    return jax.shard_map(
        shards,
        mesh=mesh,
        in_specs=(
            P("cam", "frame", None, None),
            P("cam", "frame"),
            P("cam", None),
            P(),
            P(),
            P(),
            P(),
            P(),
        ),
        out_specs=P("cam", "frame", None, None),
        check_vma=False,
    )
```

```python
import functools
import math

import jax
import jax.numpy as jnp
from jax import lax
from jax.experimental import pallas as pl
from jax.experimental.pallas import tpu as pltpu
from jax.sharding import PartitionSpec as P

HEADS = 8
MESH = pl.DeviceIdType.MESH

epsilon = 1e-06
row_tokens = 64
minus = -1e30


def normalize(values):
    values = values.astype(jnp.float32)
    mean = jnp.mean(values, axis=-1, keepdims=True)
    centred = values - mean
    variance = jnp.mean(centred * centred, axis=-1, keepdims=True)
    return (centred * lax.rsqrt(variance + epsilon)).astype(jnp.bfloat16)


def dot(a, b):
    return jnp.dot(a, b, preferred_element_type=jnp.float32)


def dot_t(a, b):
    return lax.dot_general(a, b, (((1,), (1,)), ((), ())), preferred_element_type=jnp.float32)


class Heads:
    def __init__(self, inner):
        self.inner = inner
        self.size = inner // HEADS
        self.scale = self.size ** (-0.5) * math.log2(math.e)
        self.windows = []
        for h in range(HEADS):
            lo = h * self.size
            start = lo // 128 * 128
            end = min(-(-(lo + self.size) // 128) * 128, inner)
            self.windows.append((start, end))

    def mask(self, h, dtype):
        start, end = self.windows[h]
        lane = lax.broadcasted_iota(jnp.int32, (1, end - start), 1) + start
        inside = (lane >= h * self.size) & (lane < (h + 1) * self.size)
        return jnp.where(inside, 1.0, 0.0).astype(dtype)

    def gather(self, results):
        tiles = {}
        for h, result in enumerate(results):
            start, end = self.windows[h]
            for at in range(start, end, 128):
                piece = result[:, at - start : min(at + 128, end) - start]
                tiles[at] = tiles[at] + piece if at in tiles else piece
        return jnp.concatenate([tiles[at] for at in sorted(tiles)], axis=1)


def block_kernel(
    peers,
    cam_peers,
    counts,
    neighbours,
    tokens_hbm,
    side_keys,
    cross_qkv_hbm,
    cross_out_hbm,
    time_qkv_hbm,
    time_out_hbm,
    out,
    tokens,
    cross_qkv,
    cross_out,
    time_qkv,
    time_out,
    edge,
    query,
    keys,
    values,
    shifted,
    sides,
    far_values,
    part,
    highest,
    total,
    mixed,
    leaving,
    arrived,
    early,
    crossed,
    late,
    incoming,
    attended,
    returned,
    count_out,
    count_in,
    count_edge,
    load_sem,
    edge_send,
    edge_recv,
    count_send,
    count_recv,
    cedge_send,
    cedge_recv,
    early_send,
    early_recv,
    go_send,
    go_recv,
    late_send,
    late_recv,
    back_send,
    back_recv,
):
    cams, token_count, width = tokens.shape
    inner = cross_out.shape[0]
    heads = Heads(inner)
    rows = token_count // peers
    me = lax.axis_index("frame")
    cam = lax.axis_index("cam")
    above = lax.rem(cam + 1, cam_peers)
    below = lax.rem(cam + cam_peers - 1, cam_peers)
    half = peers // 2
    side, place_in = lax.div(me, half), lax.rem(me, half)
    others = []
    for k in range(half):
        if k:
            others.append(side * half + lax.rem(place_in + k, half))
        others.append((1 - side) * half + lax.rem(place_in + k, half))

    loads = [
        pltpu.make_async_copy(source, target, load_sem.at[i])
        for i, (source, target) in enumerate(
            (
                (tokens_hbm, tokens),
                (cross_qkv_hbm, cross_qkv),
                (cross_out_hbm, cross_out),
                (time_qkv_hbm, time_qkv),
                (time_out_hbm, time_out),
            )
        )
    ]
    for load in loads:
        load.start()

    for c in range(cams):
        count_out[pl.ds(c, 1), :] = jnp.full((1, token_count), counts[0, c], jnp.int32)

    barrier = pltpu.get_barrier_semaphore()
    for peer in others:
        pl.semaphore_signal(barrier, inc=1, device_id={"frame": peer}, device_id_type=MESH)
    for peer in (above, below):
        pl.semaphore_signal(barrier, inc=1, device_id={"cam": peer}, device_id_type=MESH)
    pl.semaphore_wait(barrier, peers + 1)

    def remote(source, target, send, recv, device):
        return pltpu.make_async_remote_copy(
            src_ref=source,
            dst_ref=target,
            send_sem=send,
            recv_sem=recv,
            device_id=device,
            device_id_type=MESH,
        )

    edges = []
    for slot, peer in ((0, above), (1, below)):
        copy = remote(
            tokens_hbm.at[1 - slot],
            edge.at[slot],
            edge_send.at[slot],
            edge_recv.at[slot],
            {"cam": peer},
        )
        copy.start()
        edges.append(copy)
    for slot, peer in ((0, above), (1, below)):
        copy = remote(
            count_out,
            count_edge.at[slot],
            cedge_send.at[slot],
            cedge_recv.at[slot],
            {"cam": peer},
        )
        copy.start()
        edges.append(copy)

    def camera_at(step):
        return lax.rem(step + cam + 1, 2)

    def early_copy(peer):
        return remote(
            tokens_hbm.at[camera_at(1), pl.ds(pl.multiple_of(peer * rows, rows), rows)],
            early.at[me],
            early_send.at[peer],
            early_recv.at[me],
            {"frame": peer},
        )

    for peer in others:
        early_copy(peer).start()

    def count_copy(peer):
        return remote(
            count_out, count_in.at[me], count_send.at[peer], count_recv.at[me], {"frame": peer}
        )

    for peer in others:
        count_copy(peer).start()
    count_in[me] = count_out[...]

    cameras = cams * cam_peers
    first = side_keys[0:1, :].astype(jnp.float32)
    second = side_keys[1:2, :].astype(jnp.float32)
    for c in range(cams):
        lower = lax.rem(cams * cam + c + cameras - 1, cameras)
        straight = jnp.where(neighbours[c, 0] == lower, 1.0, 0.0)
        side_lower = first * straight + second * (1.0 - straight)
        side_upper = second * straight + first * (1.0 - straight)
        near, far = (side_upper, side_lower) if c == 0 else (side_lower, side_upper)
        sides[pl.ds(c, 1), :] = near
        sides[pl.ds(cams + c, 1), :] = far

    def key_value(normed, weight):
        key = dot_t(normed, weight[inner : 2 * inner, :])
        value = dot_t(normed, weight[2 * inner :, :])
        return key, value.astype(jnp.bfloat16)

    loads[0].wait()
    normed = normalize(tokens[...].reshape(cams * token_count, width))
    loads[1].wait()
    shape = (cams, token_count, inner)
    query[...] = dot_t(normed, cross_qkv[:inner, :]).astype(jnp.bfloat16).reshape(shape)
    key, value = key_value(normed, cross_qkv)
    keys[...] = key.astype(jnp.bfloat16).reshape(shape)
    values[...] = value.reshape(shape)

    def bias_of(row):
        lane = lax.broadcasted_iota(jnp.int32, row.shape, 1)
        return jnp.where(lane < row_tokens * row, 0.0, minus)

    def with_side(key, side):
        return (key.astype(jnp.float32) + side).astype(jnp.bfloat16)

    def local_part(c):
        near = 1 - c
        shifted[...] = with_side(keys[near], sides[pl.ds(c, 1), :])
        own_bias = bias_of(count_out[pl.ds(c, 1), :])
        near_bias = bias_of(count_out[pl.ds(near, 1), :])
        for h in range(HEADS):
            start, end = heads.windows[h]
            q = query[c, :, start:end] * heads.mask(h, jnp.bfloat16)
            own = dot_t(q, keys[c, :, start:end]) * heads.scale + own_bias
            other = dot_t(q, shifted[:, start:end]) * heads.scale + near_bias
            top = jnp.max(jnp.maximum(own, other), axis=1, keepdims=True)
            own = jnp.exp2(own - top)
            other = jnp.exp2(other - top)
            highest[c, h] = top
            total[c, h] = jnp.sum(own + other, axis=1, keepdims=True)
            part[c, h, :, : end - start] = dot(
                own.astype(jnp.bfloat16), values[c, :, start:end]
            ) + dot(other.astype(jnp.bfloat16), values[near, :, start:end])

    def go_copy(peer):
        return remote(
            leaving.at[peer], arrived.at[me], go_send.at[peer], go_recv.at[me], {"frame": peer}
        )

    def late_copy(peer):
        return remote(
            crossed.at[peer], late.at[me], late_send.at[peer], late_recv.at[me], {"frame": peer}
        )

    def back_copy(c, peer):
        return remote(
            attended.at[c, peer],
            returned.at[c, me],
            back_send.at[c, peer],
            back_recv.at[c, me],
            {"frame": peer},
        )

    def landed(buffer, sem, *at):
        remote(buffer.at[at], buffer.at[at], sem.at[at], sem.at[at], {"frame": at[-1]}).wait_recv()

    loads[2].wait()

    def cross_part(step, carry):
        c = camera_at(step)
        local_part(c)
        remote(
            edge.at[c], edge.at[c], edge_recv.at[c], edge_recv.at[c], {"cam": above}
        ).wait_recv()
        remote(
            count_edge.at[c], count_edge.at[c], cedge_recv.at[c], cedge_recv.at[c], {"cam": above}
        ).wait_recv()
        key, value = key_value(normalize(edge[c]), cross_qkv)
        shifted[...] = with_side(key.astype(jnp.bfloat16), sides[pl.ds(cams + c, 1), :])
        far_values[...] = value
        bias = bias_of(count_edge[c, pl.ds(1 - c, 1), :])
        results = []
        for h in range(HEADS):
            start, end = heads.windows[h]
            q = query[c, :, start:end] * heads.mask(h, jnp.bfloat16)
            scores = dot_t(q, shifted[:, start:end]) * heads.scale + bias
            before = highest[c, h]
            top = jnp.maximum(before, jnp.max(scores, axis=1, keepdims=True))
            scores = jnp.exp2(scores - top)
            shrink = jnp.exp2(before - top)
            whole = total[c, h] * shrink + jnp.sum(scores, axis=1, keepdims=True)
            result = part[c, h, :, : end - start] * shrink + dot(
                scores.astype(jnp.bfloat16), far_values[:, start:end]
            )
            results.append(result * (1.0 / whole) * heads.mask(h, jnp.float32))
        result = heads.gather(results).astype(jnp.bfloat16)
        sum_ = (dot(result, cross_out[...]) + tokens[c].astype(jnp.float32)).astype(jnp.bfloat16)
        mixed[c] = sum_

        @pl.when(step == 0)
        def _():
            leaving[...] = normalize(sum_).reshape(peers, rows, width)
            for peer in others:
                go_copy(peer).start()
            arrived[me] = leaving[me]

        @pl.when(step == 1)
        def _():
            crossed[...] = result.reshape(peers, rows, inner)
            for peer in others:
                late_copy(peer).start()
            late[me] = crossed[me]
            early[me] = tokens[c, pl.ds(pl.multiple_of(me * rows, rows), rows), :]

        return carry

    lax.fori_loop(0, cams, cross_part, 0)

    for peer in others:
        remote(
            count_in.at[peer],
            count_in.at[peer],
            count_recv.at[peer],
            count_recv.at[peer],
            {"frame": peer},
        ).wait_recv()
    loads[3].wait()

    def time_part(step, carry):
        c = camera_at(step)
        row = lax.broadcasted_iota(jnp.int32, (token_count, 1), 0)
        lane = lax.broadcasted_iota(jnp.int32, (1, token_count), 1)
        count = jnp.zeros((1, token_count), jnp.int32)
        row_frame = jnp.zeros((token_count, 1), jnp.int32)
        lane_frame = jnp.zeros((1, token_count), jnp.int32)
        for g in range(peers):
            here = (lane >= g * rows) & (lane < (g + 1) * rows)
            count = jnp.where(here, count_in[g, pl.ds(c, 1), :], count)
            if g:
                row_frame = row_frame + jnp.where(row >= g * rows, 1, 0)
                lane_frame = lane_frame + jnp.where(lane >= g * rows, 1, 0)
        place = lane - lane_frame * rows
        valid = jnp.where(me * rows + place < row_tokens * count, 1, 0)
        same_place = (row - row_frame * rows) == place
        seen = jnp.where(row_frame == lane_frame, 1, valid)
        bias = jnp.where(same_place, jnp.where(seen == 1, 0.0, minus), minus)

        @pl.when(step == 0)
        def _():
            for peer in others:
                landed(arrived, go_recv, peer)
            incoming[...] = arrived[...].reshape(token_count, width)

        @pl.when(step == 1)
        def _():
            for peer in others:
                landed(early, early_recv, peer)
                landed(late, late_recv, peer)
            again = dot(late[...].reshape(token_count, inner), cross_out[...])
            again = again + early[...].reshape(token_count, width).astype(jnp.float32)
            incoming[...] = normalize(again.astype(jnp.bfloat16))

        x = incoming[...]
        query[0] = dot_t(x, time_qkv[:inner, :]).astype(jnp.bfloat16)
        key, value = key_value(x, time_qkv)
        keys[0] = key.astype(jnp.bfloat16)
        values[0] = value
        results = []
        for h in range(HEADS):
            start, end = heads.windows[h]
            q = query[0, :, start:end] * heads.mask(h, jnp.bfloat16)
            scores = dot_t(q, keys[0, :, start:end]) * heads.scale + bias
            scores = jnp.exp2(scores - jnp.max(scores, axis=1, keepdims=True))
            whole = jnp.sum(scores, axis=1, keepdims=True)
            result = dot(scores.astype(jnp.bfloat16), values[0, :, start:end])
            results.append(result * (1.0 / whole) * heads.mask(h, jnp.float32))
        result = heads.gather(results).astype(jnp.bfloat16)
        attended[c] = result.reshape(peers, rows, inner)
        for peer in others:
            back_copy(c, peer).start()
        returned[c, me] = attended[c, me]
        return carry

    lax.fori_loop(0, cams, time_part, 0)
    loads[4].wait()

    def last_part(step, carry):
        c = camera_at(step)
        for peer in others:
            landed(returned, back_recv, c, peer)
        x = returned[c].reshape(token_count, inner)
        out[c] = (dot(x, time_out[...]) + mixed[c].astype(jnp.float32)).astype(jnp.bfloat16)
        return carry

    lax.fori_loop(0, cams, last_part, 0)

    for copy in edges:
        copy.wait_send()
    for peer in others:
        count_copy(peer).wait_send()
        early_copy(peer).wait_send()
        go_copy(peer).wait_send()
        late_copy(peer).wait_send()
        for c in range(cams):
            back_copy(c, peer).wait_send()


def whole_block(
    tokens, counts, neighbours, side_keys, cross_qkv, cross_out, time_qkv, time_out
):
    cams, frames, token_count, width = tokens.shape
    inner = cross_out.shape[0]
    peers = lax.axis_size("frame")
    cam_peers = lax.axis_size("cam")
    rows = token_count // peers
    bf16, f32 = jnp.bfloat16, jnp.float32
    vmem, smem, hbm = (
        pl.BlockSpec(memory_space=space) for space in (pltpu.VMEM, pltpu.SMEM, pl.ANY)
    )
    dma = pltpu.SemaphoreType.DMA
    scratch = [
        pltpu.VMEM((cams, token_count, width), bf16),
        pltpu.VMEM(cross_qkv.shape[::-1], bf16),
        pltpu.VMEM(cross_out.shape, bf16),
        pltpu.VMEM(time_qkv.shape[::-1], bf16),
        pltpu.VMEM(time_out.shape, bf16),
        pltpu.VMEM((2, token_count, width), bf16),
        pltpu.VMEM((cams, token_count, inner), bf16),
        pltpu.VMEM((cams, token_count, inner), bf16),
        pltpu.VMEM((cams, token_count, inner), bf16),
        pltpu.VMEM((token_count, inner), bf16),
        pltpu.VMEM((8, inner), f32),
        pltpu.VMEM((token_count, inner), bf16),
        pltpu.VMEM((cams, HEADS, token_count, 256), f32),
        pltpu.VMEM((cams, HEADS, token_count, 1), f32),
        pltpu.VMEM((cams, HEADS, token_count, 1), f32),
        pltpu.VMEM((cams, token_count, width), bf16),
        pltpu.VMEM((peers, rows, width), bf16),
        pltpu.VMEM((peers, rows, width), bf16),
        pltpu.VMEM((peers, rows, width), bf16),
        pltpu.VMEM((peers, rows, inner), bf16),
        pltpu.VMEM((peers, rows, inner), bf16),
        pltpu.VMEM((token_count, width), bf16),
        pltpu.VMEM((cams, peers, rows, inner), bf16),
        pltpu.VMEM((cams, peers, rows, inner), bf16),
        pltpu.VMEM((8, token_count), jnp.int32),
        pltpu.VMEM((peers, 8, token_count), jnp.int32),
        pltpu.VMEM((2, 8, token_count), jnp.int32),
        dma((5,)),
        dma((2,)),
        dma((2,)),
        dma((peers,)),
        dma((peers,)),
        dma((2,)),
        dma((2,)),
        dma((peers,)),
        dma((peers,)),
        dma((peers,)),
        dma((peers,)),
        dma((peers,)),
        dma((peers,)),
        dma((cams, peers)),
        dma((cams, peers)),
    ]
    result = pl.pallas_call(
        functools.partial(block_kernel, peers, cam_peers),
        out_shape=jax.ShapeDtypeStruct((cams, token_count, width), bf16),
        in_specs=[smem, smem, hbm, vmem, hbm, hbm, hbm, hbm],
        out_specs=vmem,
        scratch_shapes=scratch,
        compiler_params=pltpu.CompilerParams(
            collective_id=0, has_side_effects=True, vmem_limit_bytes=58 * 2**20
        ),
    )(
        counts.T,
        neighbours,
        tokens.reshape(cams, token_count, width),
        side_keys,
        cross_qkv.T,
        cross_out,
        time_qkv.T,
        time_out,
    )
    return result.reshape(tokens.shape)


def passed_along(x, axis, by):
    peers = lax.axis_size(axis)
    return lax.ppermute(x, axis, [(i, (i + by) % peers) for i in range(peers)])


def project(normed, weight):
    flat = normed.reshape(-1, normed.shape[-1])
    result = jnp.dot(flat, weight, preferred_element_type=jnp.float32)
    return result.reshape(normed.shape[:-1] + (weight.shape[1],))


def softmax_rows(scores, allowed):
    masked = jnp.where(allowed, scores, -1e30)
    highest = jnp.max(masked, axis=-1, keepdims=True)
    expo = jnp.exp(masked - highest)
    return (expo / jnp.sum(expo, axis=-1, keepdims=True)).astype(jnp.bfloat16)


def temporal_tail(projected, arrived, time_out):
    cams_here, frames, places, _ = projected.shape
    inner = time_out.shape[0]
    head_size = inner // HEADS
    query_heads = projected[..., :inner].reshape(cams_here, frames, places, HEADS, head_size)
    key_heads = projected[..., inner : 2 * inner].reshape(
        cams_here, frames, places, HEADS, head_size
    )
    value_heads = projected[..., 2 * inner :].reshape(cams_here, frames, places, HEADS, head_size)
    scores = jnp.einsum(
        "cfphd,cgphd->cphfg", query_heads, key_heads, preferred_element_type=jnp.float32
    ) * head_size ** (-0.5)
    allowed = (jnp.transpose(arrived, (0, 2, 1)) > 0.5)[:, :, None, None, :]
    allowed = allowed | jnp.eye(frames, dtype=jnp.bool_)[None, None, None]
    probs = softmax_rows(scores, allowed)
    attended = jnp.einsum(
        "cphfg,cgphd->cfphd", probs, value_heads, preferred_element_type=jnp.float32
    )
    attended = attended.astype(jnp.bfloat16).reshape(cams_here, frames, places, inner)
    returned = lax.all_to_all(attended, "frame", split_axis=1, concat_axis=2, tiled=True)
    return project(returned, time_out)


def plain_block(tokens, counts, neighbours, side_keys, cross_qkv, cross_out, time_qkv, time_out):
    cam_here, frames_here, token_count, width = tokens.shape
    inner = cross_out.shape[0]
    head_size = inner // HEADS
    position = lax.broadcasted_iota(jnp.int32, (cam_here, frames_here, token_count), 2)
    valid = (position < row_tokens * counts[:, :, None]).astype(jnp.bfloat16)
    projected = project(normalize(tokens), cross_qkv).astype(jnp.bfloat16)
    query = projected[..., :inner]
    keys = projected[..., inner : 2 * inner]
    values = projected[..., 2 * inner :]
    left_keys, left_values, left_valid = passed_along((keys[-1], values[-1], valid[-1]), "cam", 1)
    right_keys, right_values, right_valid = passed_along((keys[0], values[0], valid[0]), "cam", -1)
    lower_keys = jnp.concatenate([left_keys[None], keys[:-1]], axis=0)
    lower_values = jnp.concatenate([left_values[None], values[:-1]], axis=0)
    lower_valid = jnp.concatenate([left_valid[None], valid[:-1]], axis=0)
    upper_keys = jnp.concatenate([keys[1:], right_keys[None]], axis=0)
    upper_values = jnp.concatenate([values[1:], right_values[None]], axis=0)
    upper_valid = jnp.concatenate([valid[1:], right_valid[None]], axis=0)
    cameras = cam_here * lax.axis_size("cam")
    cam_ids = cam_here * lax.axis_index("cam") + jnp.arange(cam_here, dtype=jnp.int32)
    first_lower = neighbours[:, 0] == (cam_ids - 1) % cameras
    side_lower = jnp.where(first_lower[:, None], side_keys[0][None], side_keys[1][None]).astype(
        jnp.float32
    )
    side_upper = jnp.where(first_lower[:, None], side_keys[1][None], side_keys[0][None]).astype(
        jnp.float32
    )
    lower_keys = (lower_keys.astype(jnp.float32) + side_lower[:, None, None, :]).astype(
        jnp.bfloat16
    )
    upper_keys = (upper_keys.astype(jnp.float32) + side_upper[:, None, None, :]).astype(
        jnp.bfloat16
    )
    all_keys = jnp.concatenate([keys, lower_keys, upper_keys], axis=2)
    all_values = jnp.concatenate([values, lower_values, upper_values], axis=2)
    all_valid = jnp.concatenate([valid, lower_valid, upper_valid], axis=2)
    items = cam_here * frames_here
    query_heads = query.reshape(items, token_count, HEADS, head_size)
    key_heads = all_keys.reshape(items, 3 * token_count, HEADS, head_size)
    value_heads = all_values.reshape(items, 3 * token_count, HEADS, head_size)
    scores = jnp.einsum(
        "bqhd,bkhd->bhqk", query_heads, key_heads, preferred_element_type=jnp.float32
    ) * head_size ** (-0.5)
    allowed = (all_valid.reshape(items, 3 * token_count) > 0.5)[:, None, None, :]
    probs = softmax_rows(scores, allowed)
    attended = jnp.einsum("bhqk,bkhd->bqhd", probs, value_heads, preferred_element_type=jnp.float32)
    attended = attended.astype(jnp.bfloat16).reshape(cam_here, frames_here, token_count, inner)
    mixed = (project(attended, cross_out) + tokens.astype(jnp.float32)).astype(jnp.bfloat16)
    normed = lax.all_to_all(normalize(mixed), "frame", split_axis=2, concat_axis=1, tiled=True)
    temporal = temporal_tail(
        project(normed, time_qkv).astype(jnp.bfloat16),
        lax.all_to_all(valid, "frame", split_axis=2, concat_axis=1, tiled=True),
        time_out,
    )
    return (temporal + mixed.astype(jnp.float32)).astype(jnp.bfloat16)


def shards(tokens, counts, neighbours, side_keys, cross_qkv, cross_out, time_qkv, time_out):
    cams, frames, token_count, _ = tokens.shape
    peers = lax.axis_size("frame")
    fits = (
        cams == 2
        and frames == 1
        and lax.axis_size("cam") > 2
        and token_count == 256
        and token_count % (16 * peers) == 0
    )
    chosen = whole_block if fits else plain_block
    return chosen(
        tokens, counts, neighbours, side_keys, cross_qkv, cross_out, time_qkv, time_out
    )


def solution(mesh):
    return jax.shard_map(
        shards,
        mesh=mesh,
        in_specs=(
            P("cam", "frame", None, None),
            P("cam", "frame"),
            P("cam", None),
            P(),
            P(),
            P(),
            P(),
            P(),
        ),
        out_specs=P("cam", "frame", None, None),
        check_vma=False,
    )
```

```python
import functools
import math

import jax
import jax.numpy as jnp
from jax import lax
from jax.experimental import pallas as pl
from jax.experimental.pallas import tpu as pltpu
from jax.sharding import PartitionSpec as P

HEADS = 8
MESH = pl.DeviceIdType.MESH

epsilon = 1e-06
row_tokens = 64
minus = -1e30


def normalize(values):
    values = values.astype(jnp.float32)
    mean = jnp.mean(values, axis=-1, keepdims=True)
    centred = values - mean
    variance = jnp.mean(centred * centred, axis=-1, keepdims=True)
    return (centred * lax.rsqrt(variance + epsilon)).astype(jnp.bfloat16)


def dot(a, b):
    return jnp.dot(a, b, preferred_element_type=jnp.float32)


def dot_t(a, b):
    return lax.dot_general(a, b, (((1,), (1,)), ((), ())), preferred_element_type=jnp.float32)


class Heads:
    def __init__(self, inner):
        self.inner = inner
        self.size = inner // HEADS
        self.scale = self.size ** (-0.5) * math.log2(math.e)
        self.windows = []
        for h in range(HEADS):
            lo = h * self.size
            start = lo // 128 * 128
            end = min(-(-(lo + self.size) // 128) * 128, inner)
            self.windows.append((start, end))

    def mask(self, h, dtype):
        start, end = self.windows[h]
        lane = lax.broadcasted_iota(jnp.int32, (1, end - start), 1) + start
        inside = (lane >= h * self.size) & (lane < (h + 1) * self.size)
        return jnp.where(inside, 1.0, 0.0).astype(dtype)

    def gather(self, results):
        tiles = {}
        for h, result in enumerate(results):
            start, end = self.windows[h]
            for at in range(start, end, 128):
                piece = result[:, at - start : min(at + 128, end) - start]
                tiles[at] = tiles[at] + piece if at in tiles else piece
        return jnp.concatenate([tiles[at] for at in sorted(tiles)], axis=1)


def block_kernel(
    peers,
    cam_peers,
    counts,
    neighbours,
    tokens_hbm,
    side_keys,
    cross_qkv_hbm,
    cross_out_hbm,
    time_qkv_hbm,
    time_out_hbm,
    out,
    tokens,
    cross_qkv,
    cross_out,
    time_qkv,
    time_out,
    edge,
    query,
    keys,
    values,
    shifted,
    sides,
    far_values,
    normal,
    mixed,
    leaving,
    arrived,
    early,
    crossed,
    late,
    incoming,
    attended,
    returned,
    count_out,
    count_in,
    count_edge,
    load_sem,
    edge_send,
    edge_recv,
    count_send,
    count_recv,
    cedge_send,
    cedge_recv,
    early_send,
    early_recv,
    go_send,
    go_recv,
    late_send,
    late_recv,
    back_send,
    back_recv,
):
    cams, token_count, width = tokens.shape
    inner = cross_out.shape[0]
    heads = Heads(inner)
    rows = token_count // peers
    me = lax.axis_index("frame")
    cam = lax.axis_index("cam")
    above = lax.rem(cam + 1, cam_peers)
    below = lax.rem(cam + cam_peers - 1, cam_peers)
    half = peers // 2
    side, place_in = lax.div(me, half), lax.rem(me, half)
    others = []
    for k in range(half):
        if k:
            others.append(side * half + lax.rem(place_in + k, half))
        others.append((1 - side) * half + lax.rem(place_in + k, half))

    loads = [
        pltpu.make_async_copy(source, target, load_sem.at[i])
        for i, (source, target) in enumerate(
            (
                (tokens_hbm, tokens),
                (cross_qkv_hbm, cross_qkv),
                (cross_out_hbm, cross_out),
                (time_qkv_hbm, time_qkv),
                (time_out_hbm, time_out),
            )
        )
    ]
    for load in loads:
        load.start()

    for c in range(cams):
        count_out[pl.ds(c, 1), :] = jnp.full((1, token_count), counts[0, c], jnp.int32)

    barrier = pltpu.get_barrier_semaphore()
    for peer in others:
        pl.semaphore_signal(barrier, inc=1, device_id={"frame": peer}, device_id_type=MESH)
    for peer in (above, below):
        pl.semaphore_signal(barrier, inc=1, device_id={"cam": peer}, device_id_type=MESH)
    pl.semaphore_wait(barrier, peers + 1)

    def remote(source, target, send, recv, device):
        return pltpu.make_async_remote_copy(
            src_ref=source,
            dst_ref=target,
            send_sem=send,
            recv_sem=recv,
            device_id=device,
            device_id_type=MESH,
        )

    edges = []
    for slot, peer in ((0, above), (1, below)):
        copy = remote(
            tokens_hbm.at[1 - slot],
            edge.at[slot],
            edge_send.at[slot],
            edge_recv.at[slot],
            {"cam": peer},
        )
        copy.start()
        edges.append(copy)
    for slot, peer in ((0, above), (1, below)):
        copy = remote(
            count_out,
            count_edge.at[slot],
            cedge_send.at[slot],
            cedge_recv.at[slot],
            {"cam": peer},
        )
        copy.start()
        edges.append(copy)

    def camera_at(step):
        return lax.rem(step + cam + 1, 2)

    def early_copy(peer):
        return remote(
            tokens_hbm.at[camera_at(1), pl.ds(pl.multiple_of(peer * rows, rows), rows)],
            early.at[me],
            early_send.at[peer],
            early_recv.at[me],
            {"frame": peer},
        )

    for peer in others:
        early_copy(peer).start()

    def count_copy(peer):
        return remote(
            count_out, count_in.at[me], count_send.at[peer], count_recv.at[me], {"frame": peer}
        )

    for peer in others:
        count_copy(peer).start()
    count_in[me] = count_out[...]

    cameras = cams * cam_peers
    first = side_keys[0:1, :].astype(jnp.float32)
    second = side_keys[1:2, :].astype(jnp.float32)
    for c in range(cams):
        lower = lax.rem(cams * cam + c + cameras - 1, cameras)
        straight = jnp.where(neighbours[c, 0] == lower, 1.0, 0.0)
        side_lower = first * straight + second * (1.0 - straight)
        side_upper = second * straight + first * (1.0 - straight)
        near, far = (side_upper, side_lower) if c == 0 else (side_lower, side_upper)
        sides[pl.ds(c, 1), :] = near
        sides[pl.ds(cams + c, 1), :] = far

    def key_value(normed, weight):
        key = dot_t(normed, weight[inner : 2 * inner, :])
        value = dot_t(normed, weight[2 * inner :, :])
        return key, value.astype(jnp.bfloat16)

    loads[0].wait()
    normed = normalize(tokens[...].reshape(cams * token_count, width))
    normal[...] = normed.reshape(cams, token_count, width)
    loads[1].wait()
    shape = (cams, token_count, inner)
    key, value = key_value(normed, cross_qkv)
    keys[...] = key.astype(jnp.bfloat16).reshape(shape)
    values[...] = value.reshape(shape)

    def bias_of(row):
        lane = lax.broadcasted_iota(jnp.int32, row.shape, 1)
        return jnp.where(lane < row_tokens * row, 0.0, minus)

    def with_side(key, side):
        return (key.astype(jnp.float32) + side).astype(jnp.bfloat16)

    def go_copy(peer):
        return remote(
            leaving.at[peer], arrived.at[me], go_send.at[peer], go_recv.at[me], {"frame": peer}
        )

    def late_copy(peer):
        return remote(
            crossed.at[peer], late.at[me], late_send.at[peer], late_recv.at[me], {"frame": peer}
        )

    def back_copy(c, peer):
        return remote(
            attended.at[c, peer],
            returned.at[c, me],
            back_send.at[c, peer],
            back_recv.at[c, me],
            {"frame": peer},
        )

    def landed(buffer, sem, *at):
        remote(buffer.at[at], buffer.at[at], sem.at[at], sem.at[at], {"frame": at[-1]}).wait_recv()

    loads[2].wait()

    def cross_part(step, carry):
        c = camera_at(step)
        near = 1 - c
        query[...] = dot_t(normal[c], cross_qkv[:inner, :]).astype(jnp.bfloat16)
        shifted[0] = with_side(keys[near], sides[pl.ds(c, 1), :])
        remote(
            edge.at[c], edge.at[c], edge_recv.at[c], edge_recv.at[c], {"cam": above}
        ).wait_recv()
        remote(
            count_edge.at[c], count_edge.at[c], cedge_recv.at[c], cedge_recv.at[c], {"cam": above}
        ).wait_recv()
        key, value = key_value(normalize(edge[c]), cross_qkv)
        shifted[1] = with_side(key.astype(jnp.bfloat16), sides[pl.ds(cams + c, 1), :])
        far_values[...] = value
        biases = (
            bias_of(count_out[pl.ds(c, 1), :]),
            bias_of(count_out[pl.ds(near, 1), :]),
            bias_of(count_edge[c, pl.ds(near, 1), :]),
        )
        results = []
        for h in range(HEADS):
            start, end = heads.windows[h]
            lanes = slice(start, end)
            q = query[:, lanes] * heads.mask(h, jnp.bfloat16)
            groups = (keys[c, :, lanes], shifted[0, :, lanes], shifted[1, :, lanes])
            scores = [
                dot_t(q, group) * heads.scale + bias for group, bias in zip(groups, biases)
            ]
            top = jnp.max(functools.reduce(jnp.maximum, scores), axis=1, keepdims=True)
            scores = [jnp.exp2(score - top) for score in scores]
            whole = jnp.sum(scores[0] + scores[1] + scores[2], axis=1, keepdims=True)
            weights = [score.astype(jnp.bfloat16) for score in scores]
            result = (
                dot(weights[0], values[c, :, lanes])
                + dot(weights[1], values[near, :, lanes])
                + dot(weights[2], far_values[:, lanes])
            )
            results.append(result * (1.0 / whole) * heads.mask(h, jnp.float32))
        result = heads.gather(results).astype(jnp.bfloat16)
        sum_ = (dot(result, cross_out[...]) + tokens[c].astype(jnp.float32)).astype(jnp.bfloat16)
        mixed[c] = sum_

        @pl.when(step == 0)
        def _():
            leaving[...] = normalize(sum_).reshape(peers, rows, width)
            for peer in others:
                go_copy(peer).start()
            arrived[me] = leaving[me]

        @pl.when(step == 1)
        def _():
            crossed[...] = result.reshape(peers, rows, inner)
            for peer in others:
                late_copy(peer).start()
            late[me] = crossed[me]
            early[me] = tokens[c, pl.ds(pl.multiple_of(me * rows, rows), rows), :]

        return carry

    lax.fori_loop(0, cams, cross_part, 0)

    for peer in others:
        remote(
            count_in.at[peer],
            count_in.at[peer],
            count_recv.at[peer],
            count_recv.at[peer],
            {"frame": peer},
        ).wait_recv()
    loads[3].wait()

    def time_part(step, carry):
        c = camera_at(step)
        row = lax.broadcasted_iota(jnp.int32, (token_count, 1), 0)
        lane = lax.broadcasted_iota(jnp.int32, (1, token_count), 1)
        count = jnp.zeros((1, token_count), jnp.int32)
        row_frame = jnp.zeros((token_count, 1), jnp.int32)
        lane_frame = jnp.zeros((1, token_count), jnp.int32)
        for g in range(peers):
            here = (lane >= g * rows) & (lane < (g + 1) * rows)
            count = jnp.where(here, count_in[g, pl.ds(c, 1), :], count)
            if g:
                row_frame = row_frame + jnp.where(row >= g * rows, 1, 0)
                lane_frame = lane_frame + jnp.where(lane >= g * rows, 1, 0)
        place = lane - lane_frame * rows
        valid = jnp.where(me * rows + place < row_tokens * count, 1, 0)
        same_place = (row - row_frame * rows) == place
        seen = jnp.where(row_frame == lane_frame, 1, valid)
        bias = jnp.where(same_place, jnp.where(seen == 1, 0.0, minus), minus)

        @pl.when(step == 0)
        def _():
            for peer in others:
                landed(arrived, go_recv, peer)
            incoming[...] = arrived[...].reshape(token_count, width)

        @pl.when(step == 1)
        def _():
            for peer in others:
                landed(early, early_recv, peer)
                landed(late, late_recv, peer)
            again = dot(late[...].reshape(token_count, inner), cross_out[...])
            again = again + early[...].reshape(token_count, width).astype(jnp.float32)
            incoming[...] = normalize(again.astype(jnp.bfloat16))

        x = incoming[...]
        query[...] = dot_t(x, time_qkv[:inner, :]).astype(jnp.bfloat16)
        key, value = key_value(x, time_qkv)
        keys[0] = key.astype(jnp.bfloat16)
        values[0] = value
        results = []
        for h in range(HEADS):
            start, end = heads.windows[h]
            q = query[:, start:end] * heads.mask(h, jnp.bfloat16)
            scores = dot_t(q, keys[0, :, start:end]) * heads.scale + bias
            scores = jnp.exp2(scores - jnp.max(scores, axis=1, keepdims=True))
            whole = jnp.sum(scores, axis=1, keepdims=True)
            result = dot(scores.astype(jnp.bfloat16), values[0, :, start:end])
            results.append(result * (1.0 / whole) * heads.mask(h, jnp.float32))
        result = heads.gather(results).astype(jnp.bfloat16)
        attended[c] = result.reshape(peers, rows, inner)
        for peer in others:
            back_copy(c, peer).start()
        returned[c, me] = attended[c, me]
        return carry

    lax.fori_loop(0, cams, time_part, 0)
    loads[4].wait()

    def last_part(step, carry):
        c = camera_at(step)
        for peer in others:
            landed(returned, back_recv, c, peer)
        x = returned[c].reshape(token_count, inner)
        out[c] = (dot(x, time_out[...]) + mixed[c].astype(jnp.float32)).astype(jnp.bfloat16)
        return carry

    lax.fori_loop(0, cams, last_part, 0)

    for copy in edges:
        copy.wait_send()
    for peer in others:
        count_copy(peer).wait_send()
        early_copy(peer).wait_send()
        go_copy(peer).wait_send()
        late_copy(peer).wait_send()
        for c in range(cams):
            back_copy(c, peer).wait_send()


def whole_block(
    tokens, counts, neighbours, side_keys, cross_qkv, cross_out, time_qkv, time_out
):
    cams, frames, token_count, width = tokens.shape
    inner = cross_out.shape[0]
    peers = lax.axis_size("frame")
    cam_peers = lax.axis_size("cam")
    rows = token_count // peers
    bf16, f32 = jnp.bfloat16, jnp.float32
    vmem, smem, hbm = (
        pl.BlockSpec(memory_space=space) for space in (pltpu.VMEM, pltpu.SMEM, pl.ANY)
    )
    dma = pltpu.SemaphoreType.DMA
    scratch = [
        pltpu.VMEM((cams, token_count, width), bf16),
        pltpu.VMEM(cross_qkv.shape[::-1], bf16),
        pltpu.VMEM(cross_out.shape, bf16),
        pltpu.VMEM(time_qkv.shape[::-1], bf16),
        pltpu.VMEM(time_out.shape, bf16),
        pltpu.VMEM((2, token_count, width), bf16),
        pltpu.VMEM((token_count, inner), bf16),
        pltpu.VMEM((cams, token_count, inner), bf16),
        pltpu.VMEM((cams, token_count, inner), bf16),
        pltpu.VMEM((2, token_count, inner), bf16),
        pltpu.VMEM((8, inner), f32),
        pltpu.VMEM((token_count, inner), bf16),
        pltpu.VMEM((cams, token_count, width), bf16),
        pltpu.VMEM((cams, token_count, width), bf16),
        pltpu.VMEM((peers, rows, width), bf16),
        pltpu.VMEM((peers, rows, width), bf16),
        pltpu.VMEM((peers, rows, width), bf16),
        pltpu.VMEM((peers, rows, inner), bf16),
        pltpu.VMEM((peers, rows, inner), bf16),
        pltpu.VMEM((token_count, width), bf16),
        pltpu.VMEM((cams, peers, rows, inner), bf16),
        pltpu.VMEM((cams, peers, rows, inner), bf16),
        pltpu.VMEM((8, token_count), jnp.int32),
        pltpu.VMEM((peers, 8, token_count), jnp.int32),
        pltpu.VMEM((2, 8, token_count), jnp.int32),
        dma((5,)),
        dma((2,)),
        dma((2,)),
        dma((peers,)),
        dma((peers,)),
        dma((2,)),
        dma((2,)),
        dma((peers,)),
        dma((peers,)),
        dma((peers,)),
        dma((peers,)),
        dma((peers,)),
        dma((peers,)),
        dma((cams, peers)),
        dma((cams, peers)),
    ]
    result = pl.pallas_call(
        functools.partial(block_kernel, peers, cam_peers),
        out_shape=jax.ShapeDtypeStruct((cams, token_count, width), bf16),
        in_specs=[smem, smem, hbm, vmem, hbm, hbm, hbm, hbm],
        out_specs=vmem,
        scratch_shapes=scratch,
        compiler_params=pltpu.CompilerParams(
            collective_id=0, has_side_effects=True, vmem_limit_bytes=58 * 2**20
        ),
    )(
        counts.T,
        neighbours,
        tokens.reshape(cams, token_count, width),
        side_keys,
        cross_qkv.T,
        cross_out,
        time_qkv.T,
        time_out,
    )
    return result.reshape(tokens.shape)


def passed_along(x, axis, by):
    peers = lax.axis_size(axis)
    return lax.ppermute(x, axis, [(i, (i + by) % peers) for i in range(peers)])


def project(normed, weight):
    flat = normed.reshape(-1, normed.shape[-1])
    result = jnp.dot(flat, weight, preferred_element_type=jnp.float32)
    return result.reshape(normed.shape[:-1] + (weight.shape[1],))


def softmax_rows(scores, allowed):
    masked = jnp.where(allowed, scores, -1e30)
    highest = jnp.max(masked, axis=-1, keepdims=True)
    expo = jnp.exp(masked - highest)
    return (expo / jnp.sum(expo, axis=-1, keepdims=True)).astype(jnp.bfloat16)


def temporal_tail(projected, arrived, time_out):
    cams_here, frames, places, _ = projected.shape
    inner = time_out.shape[0]
    head_size = inner // HEADS
    query_heads = projected[..., :inner].reshape(cams_here, frames, places, HEADS, head_size)
    key_heads = projected[..., inner : 2 * inner].reshape(
        cams_here, frames, places, HEADS, head_size
    )
    value_heads = projected[..., 2 * inner :].reshape(cams_here, frames, places, HEADS, head_size)
    scores = jnp.einsum(
        "cfphd,cgphd->cphfg", query_heads, key_heads, preferred_element_type=jnp.float32
    ) * head_size ** (-0.5)
    allowed = (jnp.transpose(arrived, (0, 2, 1)) > 0.5)[:, :, None, None, :]
    allowed = allowed | jnp.eye(frames, dtype=jnp.bool_)[None, None, None]
    probs = softmax_rows(scores, allowed)
    attended = jnp.einsum(
        "cphfg,cgphd->cfphd", probs, value_heads, preferred_element_type=jnp.float32
    )
    attended = attended.astype(jnp.bfloat16).reshape(cams_here, frames, places, inner)
    returned = lax.all_to_all(attended, "frame", split_axis=1, concat_axis=2, tiled=True)
    return project(returned, time_out)


def plain_block(tokens, counts, neighbours, side_keys, cross_qkv, cross_out, time_qkv, time_out):
    cam_here, frames_here, token_count, width = tokens.shape
    inner = cross_out.shape[0]
    head_size = inner // HEADS
    position = lax.broadcasted_iota(jnp.int32, (cam_here, frames_here, token_count), 2)
    valid = (position < row_tokens * counts[:, :, None]).astype(jnp.bfloat16)
    projected = project(normalize(tokens), cross_qkv).astype(jnp.bfloat16)
    query = projected[..., :inner]
    keys = projected[..., inner : 2 * inner]
    values = projected[..., 2 * inner :]
    left_keys, left_values, left_valid = passed_along((keys[-1], values[-1], valid[-1]), "cam", 1)
    right_keys, right_values, right_valid = passed_along((keys[0], values[0], valid[0]), "cam", -1)
    lower_keys = jnp.concatenate([left_keys[None], keys[:-1]], axis=0)
    lower_values = jnp.concatenate([left_values[None], values[:-1]], axis=0)
    lower_valid = jnp.concatenate([left_valid[None], valid[:-1]], axis=0)
    upper_keys = jnp.concatenate([keys[1:], right_keys[None]], axis=0)
    upper_values = jnp.concatenate([values[1:], right_values[None]], axis=0)
    upper_valid = jnp.concatenate([valid[1:], right_valid[None]], axis=0)
    cameras = cam_here * lax.axis_size("cam")
    cam_ids = cam_here * lax.axis_index("cam") + jnp.arange(cam_here, dtype=jnp.int32)
    first_lower = neighbours[:, 0] == (cam_ids - 1) % cameras
    side_lower = jnp.where(first_lower[:, None], side_keys[0][None], side_keys[1][None]).astype(
        jnp.float32
    )
    side_upper = jnp.where(first_lower[:, None], side_keys[1][None], side_keys[0][None]).astype(
        jnp.float32
    )
    lower_keys = (lower_keys.astype(jnp.float32) + side_lower[:, None, None, :]).astype(
        jnp.bfloat16
    )
    upper_keys = (upper_keys.astype(jnp.float32) + side_upper[:, None, None, :]).astype(
        jnp.bfloat16
    )
    all_keys = jnp.concatenate([keys, lower_keys, upper_keys], axis=2)
    all_values = jnp.concatenate([values, lower_values, upper_values], axis=2)
    all_valid = jnp.concatenate([valid, lower_valid, upper_valid], axis=2)
    items = cam_here * frames_here
    query_heads = query.reshape(items, token_count, HEADS, head_size)
    key_heads = all_keys.reshape(items, 3 * token_count, HEADS, head_size)
    value_heads = all_values.reshape(items, 3 * token_count, HEADS, head_size)
    scores = jnp.einsum(
        "bqhd,bkhd->bhqk", query_heads, key_heads, preferred_element_type=jnp.float32
    ) * head_size ** (-0.5)
    allowed = (all_valid.reshape(items, 3 * token_count) > 0.5)[:, None, None, :]
    probs = softmax_rows(scores, allowed)
    attended = jnp.einsum("bhqk,bkhd->bqhd", probs, value_heads, preferred_element_type=jnp.float32)
    attended = attended.astype(jnp.bfloat16).reshape(cam_here, frames_here, token_count, inner)
    mixed = (project(attended, cross_out) + tokens.astype(jnp.float32)).astype(jnp.bfloat16)
    normed = lax.all_to_all(normalize(mixed), "frame", split_axis=2, concat_axis=1, tiled=True)
    temporal = temporal_tail(
        project(normed, time_qkv).astype(jnp.bfloat16),
        lax.all_to_all(valid, "frame", split_axis=2, concat_axis=1, tiled=True),
        time_out,
    )
    return (temporal + mixed.astype(jnp.float32)).astype(jnp.bfloat16)


def shards(tokens, counts, neighbours, side_keys, cross_qkv, cross_out, time_qkv, time_out):
    cams, frames, token_count, _ = tokens.shape
    peers = lax.axis_size("frame")
    fits = (
        cams == 2
        and frames == 1
        and lax.axis_size("cam") > 2
        and token_count == 256
        and token_count % (16 * peers) == 0
    )
    chosen = whole_block if fits else plain_block
    return chosen(
        tokens, counts, neighbours, side_keys, cross_qkv, cross_out, time_qkv, time_out
    )


def solution(mesh):
    return jax.shard_map(
        shards,
        mesh=mesh,
        in_specs=(
            P("cam", "frame", None, None),
            P("cam", "frame"),
            P("cam", None),
            P(),
            P(),
            P(),
            P(),
            P(),
        ),
        out_specs=P("cam", "frame", None, None),
        check_vma=False,
    )
```

```python
import functools
import math

import jax
import jax.numpy as jnp
from jax import lax
from jax.experimental import pallas as pl
from jax.experimental.pallas import tpu as pltpu
from jax.sharding import PartitionSpec as P

HEADS = 8
MESH = pl.DeviceIdType.MESH

epsilon = 1e-06
row_tokens = 64
minus = -1e30


def normalize(values):
    values = values.astype(jnp.float32)
    mean = jnp.mean(values, axis=-1, keepdims=True)
    centred = values - mean
    variance = jnp.mean(centred * centred, axis=-1, keepdims=True)
    return (centred * lax.rsqrt(variance + epsilon)).astype(jnp.bfloat16)


def dot(a, b):
    return jnp.dot(a, b, preferred_element_type=jnp.float32)


def dot_t(a, b):
    return lax.dot_general(a, b, (((1,), (1,)), ((), ())), preferred_element_type=jnp.float32)


class Heads:
    def __init__(self, inner):
        self.inner = inner
        self.size = inner // HEADS
        self.scale = self.size ** (-0.5) * math.log2(math.e)
        self.windows = []
        for h in range(HEADS):
            lo = h * self.size
            start = lo // 128 * 128
            end = min(-(-(lo + self.size) // 128) * 128, inner)
            self.windows.append((start, end))

    def mask(self, h, dtype):
        start, end = self.windows[h]
        lane = lax.broadcasted_iota(jnp.int32, (1, end - start), 1) + start
        inside = (lane >= h * self.size) & (lane < (h + 1) * self.size)
        return jnp.where(inside, 1.0, 0.0).astype(dtype)

    def gather(self, results):
        tiles = {}
        for h, result in enumerate(results):
            start, end = self.windows[h]
            for at in range(start, end, 128):
                piece = result[:, at - start : min(at + 128, end) - start]
                tiles[at] = tiles[at] + piece if at in tiles else piece
        return jnp.concatenate([tiles[at] for at in sorted(tiles)], axis=1)


def block_kernel(
    peers,
    cam_peers,
    counts,
    neighbours,
    tokens_hbm,
    side_keys,
    cross_qkv_hbm,
    cross_out_hbm,
    time_qkv_hbm,
    temporal_hbm,
    mixed_hbm,
    tokens,
    cross_qkv,
    cross_out,
    time_qkv,
    edge,
    query,
    keys,
    values,
    shifted,
    sides,
    far_values,
    normal,
    mixed,
    leaving,
    arrived,
    early,
    crossed,
    late,
    incoming,
    attended,
    returned,
    count_out,
    count_in,
    count_edge,
    load_sem,
    store_sem,
    edge_send,
    edge_recv,
    count_send,
    count_recv,
    cedge_send,
    cedge_recv,
    early_send,
    early_recv,
    go_send,
    go_recv,
    late_send,
    late_recv,
    back_send,
    back_recv,
):
    cams, token_count, width = tokens.shape
    inner = cross_out.shape[0]
    heads = Heads(inner)
    rows = token_count // peers
    me = lax.axis_index("frame")
    cam = lax.axis_index("cam")
    above = lax.rem(cam + 1, cam_peers)
    below = lax.rem(cam + cam_peers - 1, cam_peers)
    half = peers // 2
    side, place_in = lax.div(me, half), lax.rem(me, half)
    others = []
    for k in range(half):
        if k:
            others.append(side * half + lax.rem(place_in + k, half))
        others.append((1 - side) * half + lax.rem(place_in + k, half))

    loads = [
        pltpu.make_async_copy(source, target, load_sem.at[i])
        for i, (source, target) in enumerate(
            (
                (tokens_hbm, tokens),
                (cross_qkv_hbm, cross_qkv),
                (cross_out_hbm, cross_out),
                (time_qkv_hbm, time_qkv),
            )
        )
    ]
    for load in loads:
        load.start()

    for c in range(cams):
        count_out[pl.ds(c, 1), :] = jnp.full((1, token_count), counts[0, c], jnp.int32)

    barrier = pltpu.get_barrier_semaphore()
    for peer in others:
        pl.semaphore_signal(barrier, inc=1, device_id={"frame": peer}, device_id_type=MESH)
    for peer in (above, below):
        pl.semaphore_signal(barrier, inc=1, device_id={"cam": peer}, device_id_type=MESH)
    pl.semaphore_wait(barrier, peers + 1)

    def remote(source, target, send, recv, device):
        return pltpu.make_async_remote_copy(
            src_ref=source,
            dst_ref=target,
            send_sem=send,
            recv_sem=recv,
            device_id=device,
            device_id_type=MESH,
        )

    edges = []
    for slot, peer in ((0, above), (1, below)):
        copy = remote(
            tokens_hbm.at[1 - slot],
            edge.at[slot],
            edge_send.at[slot],
            edge_recv.at[slot],
            {"cam": peer},
        )
        copy.start()
        edges.append(copy)
    for slot, peer in ((0, above), (1, below)):
        copy = remote(
            count_out,
            count_edge.at[slot],
            cedge_send.at[slot],
            cedge_recv.at[slot],
            {"cam": peer},
        )
        copy.start()
        edges.append(copy)

    def camera_at(step):
        return lax.rem(step + cam + 1, 2)

    def early_copy(peer):
        return remote(
            tokens_hbm.at[camera_at(1), pl.ds(pl.multiple_of(peer * rows, rows), rows)],
            early.at[me],
            early_send.at[peer],
            early_recv.at[me],
            {"frame": peer},
        )

    for peer in others:
        early_copy(peer).start()

    def count_copy(peer):
        return remote(
            count_out, count_in.at[me], count_send.at[peer], count_recv.at[me], {"frame": peer}
        )

    for peer in others:
        count_copy(peer).start()
    count_in[me] = count_out[...]

    cameras = cams * cam_peers
    first = side_keys[0:1, :].astype(jnp.float32)
    second = side_keys[1:2, :].astype(jnp.float32)
    for c in range(cams):
        lower = lax.rem(cams * cam + c + cameras - 1, cameras)
        straight = jnp.where(neighbours[c, 0] == lower, 1.0, 0.0)
        side_lower = first * straight + second * (1.0 - straight)
        side_upper = second * straight + first * (1.0 - straight)
        near, far = (side_upper, side_lower) if c == 0 else (side_lower, side_upper)
        sides[pl.ds(c, 1), :] = near
        sides[pl.ds(cams + c, 1), :] = far

    def key_value(normed, weight):
        key = dot_t(normed, weight[inner : 2 * inner, :])
        value = dot_t(normed, weight[2 * inner :, :])
        return key, value.astype(jnp.bfloat16)

    loads[0].wait()
    normed = normalize(tokens[...].reshape(cams * token_count, width))
    normal[...] = normed.reshape(cams, token_count, width)
    loads[1].wait()
    shape = (cams, token_count, inner)
    key, value = key_value(normed, cross_qkv)
    keys[...] = key.astype(jnp.bfloat16).reshape(shape)
    values[...] = value.reshape(shape)

    def bias_of(row):
        lane = lax.broadcasted_iota(jnp.int32, row.shape, 1)
        return jnp.where(lane < row_tokens * row, 0.0, minus)

    def with_side(key, side):
        return (key.astype(jnp.float32) + side).astype(jnp.bfloat16)

    def mixed_store(c):
        return pltpu.make_async_copy(mixed.at[c], mixed_hbm.at[c], store_sem.at[c])

    def temporal_store(c):
        return pltpu.make_async_copy(returned.at[c], temporal_hbm.at[c], store_sem.at[cams + c])

    def go_copy(peer):
        return remote(
            leaving.at[peer], arrived.at[me], go_send.at[peer], go_recv.at[me], {"frame": peer}
        )

    def late_copy(peer):
        return remote(
            crossed.at[peer], late.at[me], late_send.at[peer], late_recv.at[me], {"frame": peer}
        )

    def back_copy(c, peer):
        return remote(
            attended.at[c, peer],
            returned.at[c, me],
            back_send.at[c, peer],
            back_recv.at[c, me],
            {"frame": peer},
        )

    def landed(buffer, sem, *at):
        remote(buffer.at[at], buffer.at[at], sem.at[at], sem.at[at], {"frame": at[-1]}).wait_recv()

    loads[2].wait()

    def cross_part(step, carry):
        c = camera_at(step)
        near = 1 - c
        query[...] = dot_t(normal[c], cross_qkv[:inner, :]).astype(jnp.bfloat16)
        shifted[0] = with_side(keys[near], sides[pl.ds(c, 1), :])
        remote(
            edge.at[c], edge.at[c], edge_recv.at[c], edge_recv.at[c], {"cam": above}
        ).wait_recv()
        remote(
            count_edge.at[c], count_edge.at[c], cedge_recv.at[c], cedge_recv.at[c], {"cam": above}
        ).wait_recv()
        key, value = key_value(normalize(edge[c]), cross_qkv)
        shifted[1] = with_side(key.astype(jnp.bfloat16), sides[pl.ds(cams + c, 1), :])
        far_values[...] = value
        biases = (
            bias_of(count_out[pl.ds(c, 1), :]),
            bias_of(count_out[pl.ds(near, 1), :]),
            bias_of(count_edge[c, pl.ds(near, 1), :]),
        )
        results = []
        for h in range(HEADS):
            start, end = heads.windows[h]
            lanes = slice(start, end)
            q = query[:, lanes] * heads.mask(h, jnp.bfloat16)
            groups = (keys[c, :, lanes], shifted[0, :, lanes], shifted[1, :, lanes])
            scores = [
                dot_t(q, group) * heads.scale + bias for group, bias in zip(groups, biases)
            ]
            top = jnp.max(functools.reduce(jnp.maximum, scores), axis=1, keepdims=True)
            scores = [jnp.exp2(score - top) for score in scores]
            whole = jnp.sum(scores[0] + scores[1] + scores[2], axis=1, keepdims=True)
            weights = [score.astype(jnp.bfloat16) for score in scores]
            result = (
                dot(weights[0], values[c, :, lanes])
                + dot(weights[1], values[near, :, lanes])
                + dot(weights[2], far_values[:, lanes])
            )
            results.append(result * (1.0 / whole) * heads.mask(h, jnp.float32))
        result = heads.gather(results).astype(jnp.bfloat16)
        sum_ = (dot(result, cross_out[...]) + tokens[c].astype(jnp.float32)).astype(jnp.bfloat16)
        mixed[c] = sum_
        mixed_store(c).start()

        @pl.when(step == 0)
        def _():
            leaving[...] = normalize(sum_).reshape(peers, rows, width)
            for peer in others:
                go_copy(peer).start()
            arrived[me] = leaving[me]

        @pl.when(step == 1)
        def _():
            crossed[...] = result.reshape(peers, rows, inner)
            for peer in others:
                late_copy(peer).start()
            late[me] = crossed[me]
            early[me] = tokens[c, pl.ds(pl.multiple_of(me * rows, rows), rows), :]

        return carry

    lax.fori_loop(0, cams, cross_part, 0)

    for peer in others:
        remote(
            count_in.at[peer],
            count_in.at[peer],
            count_recv.at[peer],
            count_recv.at[peer],
            {"frame": peer},
        ).wait_recv()
    loads[3].wait()

    def time_part(step, carry):
        c = camera_at(step)
        row = lax.broadcasted_iota(jnp.int32, (token_count, 1), 0)
        lane = lax.broadcasted_iota(jnp.int32, (1, token_count), 1)
        count = jnp.zeros((1, token_count), jnp.int32)
        row_frame = jnp.zeros((token_count, 1), jnp.int32)
        lane_frame = jnp.zeros((1, token_count), jnp.int32)
        for g in range(peers):
            here = (lane >= g * rows) & (lane < (g + 1) * rows)
            count = jnp.where(here, count_in[g, pl.ds(c, 1), :], count)
            if g:
                row_frame = row_frame + jnp.where(row >= g * rows, 1, 0)
                lane_frame = lane_frame + jnp.where(lane >= g * rows, 1, 0)
        place = lane - lane_frame * rows
        valid = jnp.where(me * rows + place < row_tokens * count, 1, 0)
        same_place = (row - row_frame * rows) == place
        seen = jnp.where(row_frame == lane_frame, 1, valid)
        bias = jnp.where(same_place, jnp.where(seen == 1, 0.0, minus), minus)

        @pl.when(step == 0)
        def _():
            for peer in others:
                landed(arrived, go_recv, peer)
            incoming[...] = arrived[...].reshape(token_count, width)

        @pl.when(step == 1)
        def _():
            for peer in others:
                landed(early, early_recv, peer)
                landed(late, late_recv, peer)
            again = dot(late[...].reshape(token_count, inner), cross_out[...])
            again = again + early[...].reshape(token_count, width).astype(jnp.float32)
            incoming[...] = normalize(again.astype(jnp.bfloat16))

        x = incoming[...]
        query[...] = dot_t(x, time_qkv[:inner, :]).astype(jnp.bfloat16)
        key, value = key_value(x, time_qkv)
        keys[0] = key.astype(jnp.bfloat16)
        values[0] = value
        results = []
        for h in range(HEADS):
            start, end = heads.windows[h]
            q = query[:, start:end] * heads.mask(h, jnp.bfloat16)
            scores = dot_t(q, keys[0, :, start:end]) * heads.scale + bias
            scores = jnp.exp2(scores - jnp.max(scores, axis=1, keepdims=True))
            whole = jnp.sum(scores, axis=1, keepdims=True)
            result = dot(scores.astype(jnp.bfloat16), values[0, :, start:end])
            results.append(result * (1.0 / whole) * heads.mask(h, jnp.float32))
        result = heads.gather(results).astype(jnp.bfloat16)
        attended[c] = result.reshape(peers, rows, inner)
        for peer in others:
            back_copy(c, peer).start()
        returned[c, me] = attended[c, me]
        return carry

    lax.fori_loop(0, cams, time_part, 0)

    def last_part(step, carry):
        c = camera_at(step)
        for peer in others:
            landed(returned, back_recv, c, peer)
        temporal_store(c).start()
        return carry

    lax.fori_loop(0, cams, last_part, 0)

    for c in range(cams):
        mixed_store(c).wait()
        temporal_store(c).wait()
    for copy in edges:
        copy.wait_send()
    for peer in others:
        count_copy(peer).wait_send()
        early_copy(peer).wait_send()
        go_copy(peer).wait_send()
        late_copy(peer).wait_send()
        for c in range(cams):
            back_copy(c, peer).wait_send()


def whole_block(
    tokens, counts, neighbours, side_keys, cross_qkv, cross_out, time_qkv, time_out
):
    cams, frames, token_count, width = tokens.shape
    inner = cross_out.shape[0]
    peers = lax.axis_size("frame")
    cam_peers = lax.axis_size("cam")
    rows = token_count // peers
    bf16, f32 = jnp.bfloat16, jnp.float32
    vmem, smem, hbm = (
        pl.BlockSpec(memory_space=space) for space in (pltpu.VMEM, pltpu.SMEM, pltpu.HBM)
    )
    dma = pltpu.SemaphoreType.DMA
    scratch = [
        pltpu.VMEM((cams, token_count, width), bf16),
        pltpu.VMEM(cross_qkv.shape[::-1], bf16),
        pltpu.VMEM(cross_out.shape, bf16),
        pltpu.VMEM(time_qkv.shape[::-1], bf16),
        pltpu.VMEM((2, token_count, width), bf16),
        pltpu.VMEM((token_count, inner), bf16),
        pltpu.VMEM((cams, token_count, inner), bf16),
        pltpu.VMEM((cams, token_count, inner), bf16),
        pltpu.VMEM((2, token_count, inner), bf16),
        pltpu.VMEM((8, inner), f32),
        pltpu.VMEM((token_count, inner), bf16),
        pltpu.VMEM((cams, token_count, width), bf16),
        pltpu.VMEM((cams, token_count, width), bf16),
        pltpu.VMEM((peers, rows, width), bf16),
        pltpu.VMEM((peers, rows, width), bf16),
        pltpu.VMEM((peers, rows, width), bf16),
        pltpu.VMEM((peers, rows, inner), bf16),
        pltpu.VMEM((peers, rows, inner), bf16),
        pltpu.VMEM((token_count, width), bf16),
        pltpu.VMEM((cams, peers, rows, inner), bf16),
        pltpu.VMEM((cams, peers, rows, inner), bf16),
        pltpu.VMEM((8, token_count), jnp.int32),
        pltpu.VMEM((peers, 8, token_count), jnp.int32),
        pltpu.VMEM((2, 8, token_count), jnp.int32),
        dma((4,)),
        dma((2 * cams,)),
        dma((2,)),
        dma((2,)),
        dma((peers,)),
        dma((peers,)),
        dma((2,)),
        dma((2,)),
        dma((peers,)),
        dma((peers,)),
        dma((peers,)),
        dma((peers,)),
        dma((peers,)),
        dma((peers,)),
        dma((cams, peers)),
        dma((cams, peers)),
    ]
    temporal, mixed = pl.pallas_call(
        functools.partial(block_kernel, peers, cam_peers),
        out_shape=[
            jax.ShapeDtypeStruct((cams, peers, rows, inner), bf16),
            jax.ShapeDtypeStruct((cams, token_count, width), bf16),
        ],
        in_specs=[smem, smem, hbm, vmem, hbm, hbm, hbm],
        out_specs=[hbm, hbm],
        scratch_shapes=scratch,
        compiler_params=pltpu.CompilerParams(
            collective_id=0, has_side_effects=True, vmem_limit_bytes=57 * 2**20
        ),
    )(
        counts.T,
        neighbours,
        tokens.reshape(cams, token_count, width),
        side_keys,
        cross_qkv.T,
        cross_out,
        time_qkv.T,
    )
    result = project(temporal.reshape(cams, token_count, inner), time_out) + mixed.astype(f32)
    return result.astype(bf16).reshape(tokens.shape)


def passed_along(x, axis, by):
    peers = lax.axis_size(axis)
    return lax.ppermute(x, axis, [(i, (i + by) % peers) for i in range(peers)])


def project(normed, weight):
    flat = normed.reshape(-1, normed.shape[-1])
    result = jnp.dot(flat, weight, preferred_element_type=jnp.float32)
    return result.reshape(normed.shape[:-1] + (weight.shape[1],))


def softmax_rows(scores, allowed):
    masked = jnp.where(allowed, scores, -1e30)
    highest = jnp.max(masked, axis=-1, keepdims=True)
    expo = jnp.exp(masked - highest)
    return (expo / jnp.sum(expo, axis=-1, keepdims=True)).astype(jnp.bfloat16)


def temporal_tail(projected, arrived, time_out):
    cams_here, frames, places, _ = projected.shape
    inner = time_out.shape[0]
    head_size = inner // HEADS
    query_heads = projected[..., :inner].reshape(cams_here, frames, places, HEADS, head_size)
    key_heads = projected[..., inner : 2 * inner].reshape(
        cams_here, frames, places, HEADS, head_size
    )
    value_heads = projected[..., 2 * inner :].reshape(cams_here, frames, places, HEADS, head_size)
    scores = jnp.einsum(
        "cfphd,cgphd->cphfg", query_heads, key_heads, preferred_element_type=jnp.float32
    ) * head_size ** (-0.5)
    allowed = (jnp.transpose(arrived, (0, 2, 1)) > 0.5)[:, :, None, None, :]
    allowed = allowed | jnp.eye(frames, dtype=jnp.bool_)[None, None, None]
    probs = softmax_rows(scores, allowed)
    attended = jnp.einsum(
        "cphfg,cgphd->cfphd", probs, value_heads, preferred_element_type=jnp.float32
    )
    attended = attended.astype(jnp.bfloat16).reshape(cams_here, frames, places, inner)
    returned = lax.all_to_all(attended, "frame", split_axis=1, concat_axis=2, tiled=True)
    return project(returned, time_out)


def plain_block(tokens, counts, neighbours, side_keys, cross_qkv, cross_out, time_qkv, time_out):
    cam_here, frames_here, token_count, width = tokens.shape
    inner = cross_out.shape[0]
    head_size = inner // HEADS
    position = lax.broadcasted_iota(jnp.int32, (cam_here, frames_here, token_count), 2)
    valid = (position < row_tokens * counts[:, :, None]).astype(jnp.bfloat16)
    projected = project(normalize(tokens), cross_qkv).astype(jnp.bfloat16)
    query = projected[..., :inner]
    keys = projected[..., inner : 2 * inner]
    values = projected[..., 2 * inner :]
    left_keys, left_values, left_valid = passed_along((keys[-1], values[-1], valid[-1]), "cam", 1)
    right_keys, right_values, right_valid = passed_along((keys[0], values[0], valid[0]), "cam", -1)
    lower_keys = jnp.concatenate([left_keys[None], keys[:-1]], axis=0)
    lower_values = jnp.concatenate([left_values[None], values[:-1]], axis=0)
    lower_valid = jnp.concatenate([left_valid[None], valid[:-1]], axis=0)
    upper_keys = jnp.concatenate([keys[1:], right_keys[None]], axis=0)
    upper_values = jnp.concatenate([values[1:], right_values[None]], axis=0)
    upper_valid = jnp.concatenate([valid[1:], right_valid[None]], axis=0)
    cameras = cam_here * lax.axis_size("cam")
    cam_ids = cam_here * lax.axis_index("cam") + jnp.arange(cam_here, dtype=jnp.int32)
    first_lower = neighbours[:, 0] == (cam_ids - 1) % cameras
    side_lower = jnp.where(first_lower[:, None], side_keys[0][None], side_keys[1][None]).astype(
        jnp.float32
    )
    side_upper = jnp.where(first_lower[:, None], side_keys[1][None], side_keys[0][None]).astype(
        jnp.float32
    )
    lower_keys = (lower_keys.astype(jnp.float32) + side_lower[:, None, None, :]).astype(
        jnp.bfloat16
    )
    upper_keys = (upper_keys.astype(jnp.float32) + side_upper[:, None, None, :]).astype(
        jnp.bfloat16
    )
    all_keys = jnp.concatenate([keys, lower_keys, upper_keys], axis=2)
    all_values = jnp.concatenate([values, lower_values, upper_values], axis=2)
    all_valid = jnp.concatenate([valid, lower_valid, upper_valid], axis=2)
    items = cam_here * frames_here
    query_heads = query.reshape(items, token_count, HEADS, head_size)
    key_heads = all_keys.reshape(items, 3 * token_count, HEADS, head_size)
    value_heads = all_values.reshape(items, 3 * token_count, HEADS, head_size)
    scores = jnp.einsum(
        "bqhd,bkhd->bhqk", query_heads, key_heads, preferred_element_type=jnp.float32
    ) * head_size ** (-0.5)
    allowed = (all_valid.reshape(items, 3 * token_count) > 0.5)[:, None, None, :]
    probs = softmax_rows(scores, allowed)
    attended = jnp.einsum("bhqk,bkhd->bqhd", probs, value_heads, preferred_element_type=jnp.float32)
    attended = attended.astype(jnp.bfloat16).reshape(cam_here, frames_here, token_count, inner)
    mixed = (project(attended, cross_out) + tokens.astype(jnp.float32)).astype(jnp.bfloat16)
    normed = lax.all_to_all(normalize(mixed), "frame", split_axis=2, concat_axis=1, tiled=True)
    temporal = temporal_tail(
        project(normed, time_qkv).astype(jnp.bfloat16),
        lax.all_to_all(valid, "frame", split_axis=2, concat_axis=1, tiled=True),
        time_out,
    )
    return (temporal + mixed.astype(jnp.float32)).astype(jnp.bfloat16)


def shards(tokens, counts, neighbours, side_keys, cross_qkv, cross_out, time_qkv, time_out):
    cams, frames, token_count, _ = tokens.shape
    peers = lax.axis_size("frame")
    fits = (
        cams == 2
        and frames == 1
        and lax.axis_size("cam") > 2
        and token_count == 256
        and token_count % (16 * peers) == 0
    )
    chosen = whole_block if fits else plain_block
    return chosen(
        tokens, counts, neighbours, side_keys, cross_qkv, cross_out, time_qkv, time_out
    )


def solution(mesh):
    return jax.shard_map(
        shards,
        mesh=mesh,
        in_specs=(
            P("cam", "frame", None, None),
            P("cam", "frame"),
            P("cam", None),
            P(),
            P(),
            P(),
            P(),
            P(),
        ),
        out_specs=P("cam", "frame", None, None),
        check_vma=False,
    )
```

```python
import functools
import math

import jax
import jax.numpy as jnp
from jax import lax
from jax.experimental import pallas as pl
from jax.experimental.pallas import tpu as pltpu
from jax.sharding import PartitionSpec as P

HEADS = 8
MESH = pl.DeviceIdType.MESH

epsilon = 1e-06
row_tokens = 64
minus = -1e30


def normalize(values):
    values = values.astype(jnp.float32)
    mean = jnp.mean(values, axis=-1, keepdims=True)
    centred = values - mean
    variance = jnp.mean(centred * centred, axis=-1, keepdims=True)
    return (centred * lax.rsqrt(variance + epsilon)).astype(jnp.bfloat16)


def dot(a, b):
    return jnp.dot(a, b, preferred_element_type=jnp.float32)


def dot_t(a, b):
    return lax.dot_general(a, b, (((1,), (1,)), ((), ())), preferred_element_type=jnp.float32)


class Heads:
    def __init__(self, inner):
        self.inner = inner
        self.size = inner // HEADS
        self.scale = self.size ** (-0.5) * math.log2(math.e)
        self.windows = []
        for h in range(HEADS):
            lo = h * self.size
            start = lo // 128 * 128
            end = min(-(-(lo + self.size) // 128) * 128, inner)
            self.windows.append((start, end))

    def mask(self, h, dtype):
        start, end = self.windows[h]
        lane = lax.broadcasted_iota(jnp.int32, (1, end - start), 1) + start
        inside = (lane >= h * self.size) & (lane < (h + 1) * self.size)
        return jnp.where(inside, 1.0, 0.0).astype(dtype)

    def gather(self, results):
        tiles = {}
        for h, result in enumerate(results):
            start, end = self.windows[h]
            for at in range(start, end, 128):
                piece = result[:, at - start : min(at + 128, end) - start]
                tiles[at] = tiles[at] + piece if at in tiles else piece
        return jnp.concatenate([tiles[at] for at in sorted(tiles)], axis=1)


def block_kernel(
    peers,
    cam_peers,
    counts,
    neighbours,
    tokens_hbm,
    side_keys,
    cross_qkv_hbm,
    cross_out_hbm,
    time_qkv_hbm,
    time_out_hbm,
    out_hbm,
    tokens,
    cross_qkv,
    cross_out,
    time_qkv,
    time_out,
    edge,
    query,
    keys,
    values,
    shifted,
    sides,
    far_values,
    normal,
    mixed,
    out,
    leaving,
    arrived,
    early,
    leaving_more,
    arrived_more,
    crossed,
    late,
    incoming,
    attended,
    returned,
    count_out,
    count_in,
    count_edge,
    load_sem,
    store_sem,
    edge_send,
    edge_recv,
    count_send,
    count_recv,
    cedge_send,
    cedge_recv,
    early_send,
    early_recv,
    go_send,
    go_recv,
    late_send,
    late_recv,
    more_send,
    more_recv,
    back_send,
    back_recv,
):
    cams, token_count, width = tokens.shape
    inner = cross_out.shape[0]
    heads = Heads(inner)
    rows = token_count // peers
    some = rows // 2
    me = lax.axis_index("frame")
    cam = lax.axis_index("cam")
    above = lax.rem(cam + 1, cam_peers)
    below = lax.rem(cam + cam_peers - 1, cam_peers)
    half = peers // 2
    side, place_in = lax.div(me, half), lax.rem(me, half)
    others = []
    for k in range(half):
        if k:
            others.append(side * half + lax.rem(place_in + k, half))
        others.append((1 - side) * half + lax.rem(place_in + k, half))

    loads = [
        pltpu.make_async_copy(source, target, load_sem.at[i])
        for i, (source, target) in enumerate(
            (
                (tokens_hbm, tokens),
                (cross_qkv_hbm, cross_qkv),
                (cross_out_hbm, cross_out),
                (time_qkv_hbm, time_qkv),
                (time_out_hbm, time_out),
            )
        )
    ]
    for load in loads:
        load.start()

    for c in range(cams):
        count_out[pl.ds(c, 1), :] = jnp.full((1, token_count), counts[0, c], jnp.int32)

    barrier = pltpu.get_barrier_semaphore()
    for peer in others:
        pl.semaphore_signal(barrier, inc=1, device_id={"frame": peer}, device_id_type=MESH)
    for peer in (above, below):
        pl.semaphore_signal(barrier, inc=1, device_id={"cam": peer}, device_id_type=MESH)
    pl.semaphore_wait(barrier, peers + 1)

    def remote(source, target, send, recv, device):
        return pltpu.make_async_remote_copy(
            src_ref=source,
            dst_ref=target,
            send_sem=send,
            recv_sem=recv,
            device_id=device,
            device_id_type=MESH,
        )

    edges = []
    for slot, peer in ((0, above), (1, below)):
        copy = remote(
            tokens_hbm.at[1 - slot],
            edge.at[slot],
            edge_send.at[slot],
            edge_recv.at[slot],
            {"cam": peer},
        )
        copy.start()
        edges.append(copy)
    for slot, peer in ((0, above), (1, below)):
        copy = remote(
            count_out,
            count_edge.at[slot],
            cedge_send.at[slot],
            cedge_recv.at[slot],
            {"cam": peer},
        )
        copy.start()
        edges.append(copy)

    def camera_at(step):
        return lax.rem(step + cam + 1, 2)

    def early_copy(peer):
        return remote(
            tokens_hbm.at[camera_at(1), pl.ds(pl.multiple_of(peer * rows + some, some), some)],
            early.at[me],
            early_send.at[peer],
            early_recv.at[me],
            {"frame": peer},
        )

    for peer in others:
        early_copy(peer).start()

    def count_copy(peer):
        return remote(
            count_out, count_in.at[me], count_send.at[peer], count_recv.at[me], {"frame": peer}
        )

    for peer in others:
        count_copy(peer).start()
    count_in[me] = count_out[...]

    cameras = cams * cam_peers
    first = side_keys[0:1, :].astype(jnp.float32)
    second = side_keys[1:2, :].astype(jnp.float32)
    for c in range(cams):
        lower = lax.rem(cams * cam + c + cameras - 1, cameras)
        straight = jnp.where(neighbours[c, 0] == lower, 1.0, 0.0)
        side_lower = first * straight + second * (1.0 - straight)
        side_upper = second * straight + first * (1.0 - straight)
        near, far = (side_upper, side_lower) if c == 0 else (side_lower, side_upper)
        sides[pl.ds(c, 1), :] = near
        sides[pl.ds(cams + c, 1), :] = far

    def key_value(normed, weight):
        key = dot_t(normed, weight[inner : 2 * inner, :])
        value = dot_t(normed, weight[2 * inner :, :])
        return key, value.astype(jnp.bfloat16)

    loads[0].wait()
    normed = normalize(tokens[...].reshape(cams * token_count, width))
    normal[...] = normed.reshape(cams, token_count, width)
    loads[1].wait()
    shape = (cams, token_count, inner)
    key, value = key_value(normed, cross_qkv)
    keys[...] = key.astype(jnp.bfloat16).reshape(shape)
    values[...] = value.reshape(shape)

    def bias_of(row):
        lane = lax.broadcasted_iota(jnp.int32, row.shape, 1)
        return jnp.where(lane < row_tokens * row, 0.0, minus)

    def with_side(key, side):
        return (key.astype(jnp.float32) + side).astype(jnp.bfloat16)

    def out_store(c):
        return pltpu.make_async_copy(out.at[c], out_hbm.at[c], store_sem.at[c])

    def go_copy(peer):
        return remote(
            leaving.at[peer], arrived.at[me], go_send.at[peer], go_recv.at[me], {"frame": peer}
        )

    def more_copy(peer):
        return remote(
            leaving_more.at[peer],
            arrived_more.at[me],
            more_send.at[peer],
            more_recv.at[me],
            {"frame": peer},
        )

    def late_copy(peer):
        return remote(
            crossed.at[peer], late.at[me], late_send.at[peer], late_recv.at[me], {"frame": peer}
        )

    def back_copy(c, peer):
        return remote(
            attended.at[c, peer],
            returned.at[c, me],
            back_send.at[c, peer],
            back_recv.at[c, me],
            {"frame": peer},
        )

    def landed(buffer, sem, *at):
        remote(buffer.at[at], buffer.at[at], sem.at[at], sem.at[at], {"frame": at[-1]}).wait_recv()

    loads[2].wait()

    def cross_part(step, carry):
        c = camera_at(step)
        near = 1 - c
        query[...] = dot_t(normal[c], cross_qkv[:inner, :]).astype(jnp.bfloat16)
        shifted[0] = with_side(keys[near], sides[pl.ds(c, 1), :])
        remote(
            edge.at[c], edge.at[c], edge_recv.at[c], edge_recv.at[c], {"cam": above}
        ).wait_recv()
        remote(
            count_edge.at[c], count_edge.at[c], cedge_recv.at[c], cedge_recv.at[c], {"cam": above}
        ).wait_recv()
        key, value = key_value(normalize(edge[c]), cross_qkv)
        shifted[1] = with_side(key.astype(jnp.bfloat16), sides[pl.ds(cams + c, 1), :])
        far_values[...] = value
        biases = (
            bias_of(count_out[pl.ds(c, 1), :]),
            bias_of(count_out[pl.ds(near, 1), :]),
            bias_of(count_edge[c, pl.ds(near, 1), :]),
        )
        results = []
        for h in range(HEADS):
            start, end = heads.windows[h]
            lanes = slice(start, end)
            q = query[:, lanes] * heads.mask(h, jnp.bfloat16)
            groups = (keys[c, :, lanes], shifted[0, :, lanes], shifted[1, :, lanes])
            scores = [
                dot_t(q, group) * heads.scale + bias for group, bias in zip(groups, biases)
            ]
            top = jnp.max(functools.reduce(jnp.maximum, scores), axis=1, keepdims=True)
            scores = [jnp.exp2(score - top) for score in scores]
            whole = jnp.sum(scores[0] + scores[1] + scores[2], axis=1, keepdims=True)
            weights = [score.astype(jnp.bfloat16) for score in scores]
            result = (
                dot(weights[0], values[c, :, lanes])
                + dot(weights[1], values[near, :, lanes])
                + dot(weights[2], far_values[:, lanes])
            )
            results.append(result * (1.0 / whole) * heads.mask(h, jnp.float32))
        result = heads.gather(results).astype(jnp.bfloat16)
        sum_ = (dot(result, cross_out[...]) + tokens[c].astype(jnp.float32)).astype(jnp.bfloat16)
        mixed[c] = sum_

        @pl.when(step == 0)
        def _():
            leaving[...] = normalize(sum_).reshape(peers, rows, width)
            for peer in others:
                go_copy(peer).start()
            arrived[me] = leaving[me]

        @pl.when(step == 1)
        def _():
            crossed[...] = result.reshape(peers, rows, inner)[:, some:]
            for peer in others:
                late_copy(peer).start()
            leaving_more[...] = normalize(sum_).reshape(peers, rows, width)[:, :some]
            for peer in others:
                more_copy(peer).start()
            late[me] = crossed[me]
            early[me] = tokens[c, pl.ds(pl.multiple_of(me * rows + some, some), some), :]
            arrived_more[me] = leaving_more[me]

        return carry

    lax.fori_loop(0, cams, cross_part, 0)

    for peer in others:
        remote(
            count_in.at[peer],
            count_in.at[peer],
            count_recv.at[peer],
            count_recv.at[peer],
            {"frame": peer},
        ).wait_recv()
    loads[3].wait()

    def time_part(step, carry):
        c = camera_at(step)
        row = lax.broadcasted_iota(jnp.int32, (token_count, 1), 0)
        lane = lax.broadcasted_iota(jnp.int32, (1, token_count), 1)
        count = jnp.zeros((1, token_count), jnp.int32)
        row_frame = jnp.zeros((token_count, 1), jnp.int32)
        lane_frame = jnp.zeros((1, token_count), jnp.int32)
        for g in range(peers):
            here = (lane >= g * rows) & (lane < (g + 1) * rows)
            count = jnp.where(here, count_in[g, pl.ds(c, 1), :], count)
            if g:
                row_frame = row_frame + jnp.where(row >= g * rows, 1, 0)
                lane_frame = lane_frame + jnp.where(lane >= g * rows, 1, 0)
        place = lane - lane_frame * rows
        valid = jnp.where(me * rows + place < row_tokens * count, 1, 0)
        same_place = (row - row_frame * rows) == place
        seen = jnp.where(row_frame == lane_frame, 1, valid)
        bias = jnp.where(same_place, jnp.where(seen == 1, 0.0, minus), minus)

        @pl.when(step == 0)
        def _():
            for peer in others:
                landed(arrived, go_recv, peer)
            incoming[...] = arrived[...].reshape(token_count, width)

        @pl.when(step == 1)
        def _():
            for peer in others:
                landed(early, early_recv, peer)
                landed(late, late_recv, peer)
            again = dot(late[...].reshape(peers * some, inner), cross_out[...])
            again = again + early[...].reshape(peers * some, width).astype(jnp.float32)
            again = normalize(again.astype(jnp.bfloat16)).reshape(peers, some, width)
            for peer in others:
                landed(arrived_more, more_recv, peer)
            both = jnp.concatenate([arrived_more[...], again], axis=1)
            incoming[...] = both.reshape(token_count, width)

        x = incoming[...]
        query[...] = dot_t(x, time_qkv[:inner, :]).astype(jnp.bfloat16)
        key, value = key_value(x, time_qkv)
        keys[0] = key.astype(jnp.bfloat16)
        values[0] = value
        results = []
        for h in range(HEADS):
            start, end = heads.windows[h]
            q = query[:, start:end] * heads.mask(h, jnp.bfloat16)
            scores = dot_t(q, keys[0, :, start:end]) * heads.scale + bias
            scores = jnp.exp2(scores - jnp.max(scores, axis=1, keepdims=True))
            whole = jnp.sum(scores, axis=1, keepdims=True)
            result = dot(scores.astype(jnp.bfloat16), values[0, :, start:end])
            results.append(result * (1.0 / whole) * heads.mask(h, jnp.float32))
        result = heads.gather(results).astype(jnp.bfloat16)
        attended[c] = result.reshape(peers, rows, inner)
        for peer in others:
            back_copy(c, peer).start()
        returned[c, me] = attended[c, me]
        return carry

    lax.fori_loop(0, cams, time_part, 0)
    loads[4].wait()

    def last_part(step, carry):
        c = camera_at(step)
        for peer in others:
            landed(returned, back_recv, c, peer)
        x = returned[c].reshape(token_count, inner)
        out[c] = (dot(x, time_out[...]) + mixed[c].astype(jnp.float32)).astype(jnp.bfloat16)
        out_store(c).start()
        return carry

    lax.fori_loop(0, cams, last_part, 0)

    for c in range(cams):
        out_store(c).wait()
    for copy in edges:
        copy.wait_send()
    for peer in others:
        count_copy(peer).wait_send()
        early_copy(peer).wait_send()
        go_copy(peer).wait_send()
        late_copy(peer).wait_send()
        more_copy(peer).wait_send()
        for c in range(cams):
            back_copy(c, peer).wait_send()


def copy_kernel(pieces, source, target, sem):
    size = source.shape[0] // pieces
    copies = [
        pltpu.make_async_copy(
            source.at[pl.ds(i * size, size)], target.at[pl.ds(i * size, size)], sem.at[i]
        )
        for i in range(pieces)
    ]
    for copy in copies:
        copy.start()
    for copy in copies:
        copy.wait()


def copied(x, pieces):
    flat = x.reshape(-1, x.shape[-1])
    space = pl.BlockSpec(memory_space=pltpu.HBM)
    return pl.pallas_call(
        functools.partial(copy_kernel, pieces),
        out_shape=jax.ShapeDtypeStruct(flat.shape, flat.dtype),
        in_specs=[space],
        out_specs=space,
        scratch_shapes=[pltpu.SemaphoreType.DMA((pieces,))],
    )(flat)


def whole_block(
    tokens, counts, neighbours, side_keys, cross_qkv, cross_out, time_qkv, time_out
):
    cams, frames, token_count, width = tokens.shape
    inner = cross_out.shape[0]
    peers = lax.axis_size("frame")
    cam_peers = lax.axis_size("cam")
    rows = token_count // peers
    bf16, f32 = jnp.bfloat16, jnp.float32
    vmem, smem, hbm = (
        pl.BlockSpec(memory_space=space) for space in (pltpu.VMEM, pltpu.SMEM, pltpu.HBM)
    )
    dma = pltpu.SemaphoreType.DMA
    scratch = [
        pltpu.VMEM((cams, token_count, width), bf16),
        pltpu.VMEM(cross_qkv.shape[::-1], bf16),
        pltpu.VMEM(cross_out.shape, bf16),
        pltpu.VMEM(time_qkv.shape[::-1], bf16),
        pltpu.VMEM(time_out.shape, bf16),
        pltpu.VMEM((2, token_count, width), bf16),
        pltpu.VMEM((token_count, inner), bf16),
        pltpu.VMEM((cams, token_count, inner), bf16),
        pltpu.VMEM((cams, token_count, inner), bf16),
        pltpu.VMEM((2, token_count, inner), bf16),
        pltpu.VMEM((8, inner), f32),
        pltpu.VMEM((token_count, inner), bf16),
        pltpu.VMEM((cams, token_count, width), bf16),
        pltpu.VMEM((cams, token_count, width), bf16),
        pltpu.VMEM((cams, token_count, width), bf16),
        pltpu.VMEM((peers, rows, width), bf16),
        pltpu.VMEM((peers, rows, width), bf16),
        pltpu.VMEM((peers, rows // 2, width), bf16),
        pltpu.VMEM((peers, rows // 2, width), bf16),
        pltpu.VMEM((peers, rows // 2, width), bf16),
        pltpu.VMEM((peers, rows // 2, inner), bf16),
        pltpu.VMEM((peers, rows // 2, inner), bf16),
        pltpu.VMEM((token_count, width), bf16),
        pltpu.VMEM((cams, peers, rows, inner), bf16),
        pltpu.VMEM((cams, peers, rows, inner), bf16),
        pltpu.VMEM((8, token_count), jnp.int32),
        pltpu.VMEM((peers, 8, token_count), jnp.int32),
        pltpu.VMEM((2, 8, token_count), jnp.int32),
        dma((5,)),
        dma((cams,)),
        dma((2,)),
        dma((2,)),
        dma((peers,)),
        dma((peers,)),
        dma((2,)),
        dma((2,)),
        dma((peers,)),
        dma((peers,)),
        dma((peers,)),
        dma((peers,)),
        dma((peers,)),
        dma((peers,)),
        dma((peers,)),
        dma((peers,)),
        dma((cams, peers)),
        dma((cams, peers)),
    ]
    result = pl.pallas_call(
        functools.partial(block_kernel, peers, cam_peers),
        out_shape=jax.ShapeDtypeStruct((cams, token_count, width), bf16),
        in_specs=[smem, smem, hbm, vmem, hbm, hbm, hbm, hbm],
        out_specs=hbm,
        scratch_shapes=scratch,
        compiler_params=pltpu.CompilerParams(
            collective_id=0, has_side_effects=True, vmem_limit_bytes=58 * 2**20
        ),
    )(
        counts.T,
        neighbours,
        tokens.reshape(cams, token_count, width),
        side_keys,
        cross_qkv.T,
        cross_out,
        time_qkv.T,
        time_out,
    )
    return copied(result, 8).reshape(tokens.shape)


def passed_along(x, axis, by):
    peers = lax.axis_size(axis)
    return lax.ppermute(x, axis, [(i, (i + by) % peers) for i in range(peers)])


def project(normed, weight):
    flat = normed.reshape(-1, normed.shape[-1])
    result = jnp.dot(flat, weight, preferred_element_type=jnp.float32)
    return result.reshape(normed.shape[:-1] + (weight.shape[1],))


def softmax_rows(scores, allowed):
    masked = jnp.where(allowed, scores, -1e30)
    highest = jnp.max(masked, axis=-1, keepdims=True)
    expo = jnp.exp(masked - highest)
    return (expo / jnp.sum(expo, axis=-1, keepdims=True)).astype(jnp.bfloat16)


def temporal_tail(projected, arrived, time_out):
    cams_here, frames, places, _ = projected.shape
    inner = time_out.shape[0]
    head_size = inner // HEADS
    query_heads = projected[..., :inner].reshape(cams_here, frames, places, HEADS, head_size)
    key_heads = projected[..., inner : 2 * inner].reshape(
        cams_here, frames, places, HEADS, head_size
    )
    value_heads = projected[..., 2 * inner :].reshape(cams_here, frames, places, HEADS, head_size)
    scores = jnp.einsum(
        "cfphd,cgphd->cphfg", query_heads, key_heads, preferred_element_type=jnp.float32
    ) * head_size ** (-0.5)
    allowed = (jnp.transpose(arrived, (0, 2, 1)) > 0.5)[:, :, None, None, :]
    allowed = allowed | jnp.eye(frames, dtype=jnp.bool_)[None, None, None]
    probs = softmax_rows(scores, allowed)
    attended = jnp.einsum(
        "cphfg,cgphd->cfphd", probs, value_heads, preferred_element_type=jnp.float32
    )
    attended = attended.astype(jnp.bfloat16).reshape(cams_here, frames, places, inner)
    returned = lax.all_to_all(attended, "frame", split_axis=1, concat_axis=2, tiled=True)
    return project(returned, time_out)


def plain_block(tokens, counts, neighbours, side_keys, cross_qkv, cross_out, time_qkv, time_out):
    cam_here, frames_here, token_count, width = tokens.shape
    inner = cross_out.shape[0]
    head_size = inner // HEADS
    position = lax.broadcasted_iota(jnp.int32, (cam_here, frames_here, token_count), 2)
    valid = (position < row_tokens * counts[:, :, None]).astype(jnp.bfloat16)
    projected = project(normalize(tokens), cross_qkv).astype(jnp.bfloat16)
    query = projected[..., :inner]
    keys = projected[..., inner : 2 * inner]
    values = projected[..., 2 * inner :]
    left_keys, left_values, left_valid = passed_along((keys[-1], values[-1], valid[-1]), "cam", 1)
    right_keys, right_values, right_valid = passed_along((keys[0], values[0], valid[0]), "cam", -1)
    lower_keys = jnp.concatenate([left_keys[None], keys[:-1]], axis=0)
    lower_values = jnp.concatenate([left_values[None], values[:-1]], axis=0)
    lower_valid = jnp.concatenate([left_valid[None], valid[:-1]], axis=0)
    upper_keys = jnp.concatenate([keys[1:], right_keys[None]], axis=0)
    upper_values = jnp.concatenate([values[1:], right_values[None]], axis=0)
    upper_valid = jnp.concatenate([valid[1:], right_valid[None]], axis=0)
    cameras = cam_here * lax.axis_size("cam")
    cam_ids = cam_here * lax.axis_index("cam") + jnp.arange(cam_here, dtype=jnp.int32)
    first_lower = neighbours[:, 0] == (cam_ids - 1) % cameras
    side_lower = jnp.where(first_lower[:, None], side_keys[0][None], side_keys[1][None]).astype(
        jnp.float32
    )
    side_upper = jnp.where(first_lower[:, None], side_keys[1][None], side_keys[0][None]).astype(
        jnp.float32
    )
    lower_keys = (lower_keys.astype(jnp.float32) + side_lower[:, None, None, :]).astype(
        jnp.bfloat16
    )
    upper_keys = (upper_keys.astype(jnp.float32) + side_upper[:, None, None, :]).astype(
        jnp.bfloat16
    )
    all_keys = jnp.concatenate([keys, lower_keys, upper_keys], axis=2)
    all_values = jnp.concatenate([values, lower_values, upper_values], axis=2)
    all_valid = jnp.concatenate([valid, lower_valid, upper_valid], axis=2)
    items = cam_here * frames_here
    query_heads = query.reshape(items, token_count, HEADS, head_size)
    key_heads = all_keys.reshape(items, 3 * token_count, HEADS, head_size)
    value_heads = all_values.reshape(items, 3 * token_count, HEADS, head_size)
    scores = jnp.einsum(
        "bqhd,bkhd->bhqk", query_heads, key_heads, preferred_element_type=jnp.float32
    ) * head_size ** (-0.5)
    allowed = (all_valid.reshape(items, 3 * token_count) > 0.5)[:, None, None, :]
    probs = softmax_rows(scores, allowed)
    attended = jnp.einsum("bhqk,bkhd->bqhd", probs, value_heads, preferred_element_type=jnp.float32)
    attended = attended.astype(jnp.bfloat16).reshape(cam_here, frames_here, token_count, inner)
    mixed = (project(attended, cross_out) + tokens.astype(jnp.float32)).astype(jnp.bfloat16)
    normed = lax.all_to_all(normalize(mixed), "frame", split_axis=2, concat_axis=1, tiled=True)
    temporal = temporal_tail(
        project(normed, time_qkv).astype(jnp.bfloat16),
        lax.all_to_all(valid, "frame", split_axis=2, concat_axis=1, tiled=True),
        time_out,
    )
    return (temporal + mixed.astype(jnp.float32)).astype(jnp.bfloat16)


def shards(tokens, counts, neighbours, side_keys, cross_qkv, cross_out, time_qkv, time_out):
    cams, frames, token_count, _ = tokens.shape
    peers = lax.axis_size("frame")
    fits = (
        cams == 2
        and frames == 1
        and lax.axis_size("cam") > 2
        and token_count == 256
        and token_count % (32 * peers) == 0
    )
    chosen = whole_block if fits else plain_block
    return chosen(
        tokens, counts, neighbours, side_keys, cross_qkv, cross_out, time_qkv, time_out
    )


def solution(mesh):
    return jax.shard_map(
        shards,
        mesh=mesh,
        in_specs=(
            P("cam", "frame", None, None),
            P("cam", "frame"),
            P("cam", None),
            P(),
            P(),
            P(),
            P(),
            P(),
        ),
        out_specs=P("cam", "frame", None, None),
        check_vma=False,
    )
```
